128 devices in a mesh: expert: 8 (over x, core), dp: 16 (over y, z).
Axes of the slice: x: 4, y: 4, z: 4, core: 2. Of those that a mesh axis runs over, the one named last changes fastest.
Arguments:
- saved_inputs: bfloat16 [8, 20480, 3584], P('expert', 'dp'), may hold values from -6 to 6
- saved_cotangents: bfloat16 [8, 20480, 768], P('expert', 'dp'), may hold values from -0.109375 to 0.109375
- row_counts: int32 [8, 16, 3], P('expert'), may hold values from 1 to 640, 1280 in all within a row
- old_slots: int32 [8, 2], replicated, may hold values from 0 to 7, as said below
- new_slots: int32 [8, 2], replicated, may hold values from 0 to 7, as said below
- master: float32 [8, 3584, 768], P('expert', 'dp'), may hold values from -0.3125 to 0.3125
- first_moment: float32 [8, 3584, 768], P('expert', 'dp'), may hold values from -0.75 to 0.75
- second_moment: float32 [8, 3584, 768], P('expert', 'dp'), may hold values from 0.001 to 0.2
Outputs:
- new_master: float32 [8, 3584, 768], P('expert', 'dp')
- holder_weights: bfloat16 [16, 3584, 768], P('expert', 'dp')
- holder_first: float32 [16, 3584, 768], P('expert', 'dp')
- holder_second: float32 [16, 3584, 768], P('expert', 'dp')
The draws below stay inside these ranges and needn't reach their ends.
Inputs may be any that keep to these rules, and one draw needn't show every extreme that they name: `old_slots`: every one of the 8 experts fills 1 to 4 of the 16 slots; in every draw some expert fills 4. `new_slots`: every one of the 8 experts fills 1 to 4 of the 16 slots; in every draw some expert fills 4. `row_counts`: for each device the three entries sum to 1280 and the largest is 640.
All inputs are finite; a program needn't handle non-finite values.
Results may differ from the reference program's by a relative error of at most 0.001.
Values may be sent and summed in bfloat16 or wider, within the bound.
No kernel may reach another device: no remote copies, remote signals or barrier semaphores. Data moves between devices by JAX's collectives and lax.ppermute only.
A program may use at most 320 MiB of HBM per device.

```python
import math
import jax
import jax.numpy as jnp
import numpy as np
from jax import lax

D = 3584
H = 768
ROWS_DEV = 1280
SLOTS = 2
EXPERTS = 8
ROWS = 20480
N_DP = 16


def placement(key_base):
    groups = EXPERTS // 4
    first_key, second_key, third_key, fourth_key = jax.random.split(key_base, 4)
    patterns = jnp.array([[3, 1, 0, 0], [2, 2, 0, 0], [2, 1, 1, 0], [1, 1, 1, 1]], jnp.int32)
    chosen_rows = jax.random.randint(first_key, (groups,), 0, 4).astype(jnp.int32)
    chosen_rows = chosen_rows.at[0].set(0)
    extras = patterns[chosen_rows]
    extras = jax.random.permutation(second_key, extras, axis=1, independent=True)
    replicas = 1 + extras.reshape(EXPERTS)
    experts_order = jax.random.permutation(third_key, EXPERTS).astype(jnp.int32)
    slot_list = jnp.repeat(experts_order, replicas, total_repeat_length=EXPERTS * SLOTS)
    slot_list = jax.random.permutation(fourth_key, slot_list)
    return slot_list.reshape(EXPERTS, SLOTS).astype(jnp.int32)


def draw_old_slots(key, part):
    key = jax.random.fold_in(key, 11)
    return placement(key)


def draw_new_slots(key, part):
    key = jax.random.fold_in(key, 12)
    return placement(key)


def levels(stream_key, dims, pieces, low, largest):
    gain, own = 1.0, jax.random.fold_in(stream_key, 6)
    for dim, blocks in pieces:
        heights = jnp.exp(jax.random.uniform(jax.random.fold_in(own, dim), (blocks,), jnp.float32, low / len(pieces), largest / len(pieces)))
        gain = gain * jnp.repeat(heights, dims[dim] // blocks).reshape([-1 if axis == dim else 1 for axis in range(len(dims))])
    return gain


def length_profile(amount, total, most, slope):
    weights = [(1 << 20) // math.isqrt(grade ** slope) + 1 for grade in range(2, amount + 1)]
    surplus, holding = total - most - (amount - 1), [1] * (amount - 1)
    while surplus > 0:
        free = [i for i in range(amount - 1) if holding[i] < most]
        mass, remaining = sum([weights[i] for i in free]), surplus
        for i in free:
            addition = min(most - holding[i], max(1, remaining * weights[i] // mass), surplus)
            holding[i] = holding[i] + addition
            surplus = surplus - addition
    return np.array([most] + holding)


def uneven_parts(own_key, number_of, total, most, skew):
    if number_of == 2:
        one = jax.random.randint(own_key, (), max(1, total - most), min(most, total - 1) + 1)
        return jnp.stack([one, total - one])
    lengths = jnp.asarray(length_profile(number_of, total, most, skew), jnp.int32)
    pairs = (number_of - 1) // 2
    donor, taker = lengths[1:1 + 2 * pairs:2], lengths[2:2 + 2 * pairs:2]
    room = jnp.minimum(donor - 1, most - taker)
    shifted = jax.random.randint(jax.random.fold_in(own_key, 1), (pairs,), 0, 1 << 20) % (room + 1)
    lengths = lengths.at[1:1 + 2 * pairs:2].set(donor - shifted).at[2:2 + 2 * pairs:2].set(taker + shifted)
    return lengths[jax.random.permutation(jax.random.fold_in(own_key, 2), number_of)]


def noise(key, shape, scale, most, cuts=(), kind=jnp.bfloat16):
    gain = levels(key, shape, cuts, -0.22, 0.18) if cuts else 1.0
    result = jax.random.normal(key, shape, jnp.float32) * scale * gain
    return jnp.minimum(jnp.maximum(result, -most), most).astype(kind)


def setup_inputs(seed: int = 0) -> dict:
    seeds = jax.random.split(jax.random.key(seed), 9)
    return {
        "saved_inputs": noise(seeds[0], (EXPERTS, ROWS, D), 1.0, 6.0, ((0, 8), (1, 16))),
        "saved_cotangents": noise(seeds[1], (EXPERTS, ROWS, H), ((N_DP * ROWS_DEV) ** -0.5), 0.109375, ((0, 8), (1, 16))),
        "row_counts": jax.vmap(lambda own: uneven_parts(own, SLOTS + 1, ROWS_DEV, ROWS_DEV // 2, 2))(jax.random.split(seeds[2], EXPERTS * N_DP)).reshape((EXPERTS, N_DP, SLOTS + 1)).astype(jnp.int32),
        "old_slots": draw_old_slots(jax.random.fold_in(seeds[8], 71), 0),
        "new_slots": draw_new_slots(jax.random.fold_in(seeds[8], 71), 0),
        "master": noise(seeds[5], (EXPERTS, D, H), 0.02, 0.3125, ((0, 8), (1, 16)), jnp.float32),
        "first_moment": noise(seeds[6], (EXPERTS, D, H), 0.05, 0.75, ((0, 8), (1, 16)), jnp.float32),
        "second_moment": jnp.clip(jnp.exp(math.log(0.2) - 5.2983173 * jax.random.uniform(seeds[7], (EXPERTS, D, H), jnp.float32) ** levels(seeds[7], (EXPERTS, D, H), ((0, 8), (1, 16)), -0.2, 0.2)), 0.001, 0.2),
    }


def slot_index(counts, row_count, slot_count):
    slot_ends = jnp.cumsum(counts[:slot_count])
    row_index = jnp.arange(row_count, dtype=jnp.int32)
    return lax.optimization_barrier(jnp.sum((row_index[:, None] >= slot_ends[None, :]).astype(jnp.int32), axis=1))

def masked_cotangent(cotangent, slot_ids, slot_count):
    member = (slot_ids[:, None] == jnp.arange(slot_count, dtype=jnp.int32)[None, :]).astype(cotangent.dtype)
    return (cotangent[:, None, :] * member[:, :, None]).reshape(cotangent.shape[0], slot_count * cotangent.shape[1])

def adam_update(gradient, master, first_moment, second_moment):
    first_new = 0.9 * first_moment + 0.1 * gradient
    second_new = 0.95 * second_moment + 0.05 * gradient * gradient
    corrected = first_new / (1.0 - 0.9 ** 20) / (jnp.sqrt(second_new / (1.0 - 0.95 ** 20)) + 1e-08)
    new_master = master - 0.001 * (corrected + 0.1 * master)
    return (new_master, first_new, second_new)

def reference(saved_inputs, saved_cotangents, row_counts, old_slots, new_slots, master, first_moment, second_moment):
    experts = old_slots.shape[0]
    slot_count = old_slots.shape[1]
    width_h = saved_cotangents.shape[2]
    width_d = saved_inputs.shape[2]

    def device_ids(counts):
        return slot_index(counts, ROWS_DEV, slot_count)

    def one_index(running, index_inputs):
        saved_rows, saved_cot, counts, owners = index_inputs
        slot_ids = jax.vmap(device_ids)(counts).reshape(-1)
        masked = masked_cotangent(saved_cot, slot_ids, slot_count)
        product = jnp.dot(saved_rows.astype(jnp.float32).T, masked.astype(jnp.float32), precision=lax.Precision.HIGHEST).reshape(width_d, slot_count, width_h)
        chosen = (owners[:, None] == jnp.arange(experts, dtype=jnp.int32)[None, :]).astype(jnp.float32)
        return (running + jnp.einsum('se,dsh->edh', chosen, product, precision=lax.Precision.HIGHEST), None)
    initial = jnp.zeros((experts, width_d, width_h), jnp.float32)
    gradient, _ = lax.scan(one_index, initial, (saved_inputs, saved_cotangents, row_counts, old_slots))
    new_master, first_new, second_new = adam_update(gradient, master, first_moment, second_moment)
    flat_slots = new_slots.reshape(-1)
    holder_weights = new_master[flat_slots].astype(jnp.bfloat16)
    holder_first = first_new[flat_slots]
    holder_second = second_new[flat_slots]
    return (new_master, holder_weights, holder_first, holder_second)
```

```python
import jax
import jax.numpy as jnp
from jax import lax
from jax.experimental import pallas as pl
from jax.experimental.pallas import tpu as pltpu
from jax.sharding import PartitionSpec as P

F16 = jnp.float16
F32 = jnp.float32
NY, NZ, NX = 4, 4, 4
WINDOW = 656
SCALE = 64.0


def y_shift(d):
    return [(j, ((j // NZ + d) % NY) * NZ + j % NZ) for j in range(NY * NZ)]


def z_shift(d):
    return [(j, (j // NZ) * NZ + (j % NZ + d) % NZ) for j in range(NY * NZ)]


def x_shift(d):
    return [(e, ((e // 2 + d) % NX) * 2 + e % 2) for e in range(2 * NX)]


def core_swap():
    return [(e, e ^ 1) for e in range(2 * NX)]


def adam_update(gradient, master, first_moment, second_moment):
    first_new = 0.9 * first_moment + 0.1 * gradient
    second_new = 0.95 * second_moment + 0.05 * gradient * gradient
    corrected = first_new / (1.0 - 0.9**20) / (jnp.sqrt(second_new / (1.0 - 0.95**20)) + 1e-08)
    new_master = master - 0.001 * (corrected + 0.1 * master)
    return (new_master, first_new, second_new)


def encode_moments(m, v):
    root = jnp.sqrt(jnp.sqrt(jnp.sqrt(jnp.minimum(jnp.abs(m) * (1.0 / 0.75), 1.0))))
    qm = jnp.round(jnp.where(m < 0, -root, root) * 32767.0).astype(jnp.int32)
    qv = jnp.round(jnp.sqrt(jnp.clip(v * 5.0, 0.0, 1.0)) * 65535.0).astype(jnp.int32)
    return qm * 65536 + qv


def decode_moments(code):
    qm = lax.shift_right_arithmetic(code, jnp.int32(16)).astype(F32) * (1.0 / 32767.0)
    qv = (code & jnp.int32(0xFFFF)).astype(F32) * (1.0 / 65535.0)
    m2 = qm * qm
    m4 = m2 * m2
    m8 = m4 * m4 * 0.75
    return jnp.where(qm < 0, -m8, m8), qv * qv * 0.2


def ring_sums(pieces, shifts):
    up, down = shifts[1], shifts[-1]
    far_up = lax.ppermute(pieces[2][0], "dp", up)
    far_down = lax.ppermute(pieces[2][1], "dp", down)
    raw_up = lax.ppermute(pieces[1][1], "dp", up)
    raw_down = lax.ppermute(pieces[3][0], "dp", down)
    both_up = lax.ppermute((pieces[1][0].astype(F32) + far_up.astype(F32)).astype(F16), "dp", up)
    both_down = lax.ppermute(
        (pieces[3][1].astype(F32) + far_down.astype(F32)).astype(F16), "dp", down
    )
    first = pieces[0][0].astype(F32) + both_up.astype(F32) + raw_down.astype(F32)
    second = pieces[0][1].astype(F32) + raw_up.astype(F32) + both_down.astype(F32)
    return first, second


def last_sums(halves, me, shifts):
    total = jnp.concatenate([(h * 0.5).astype(F16) for h in halves], -1)

    def block(d):
        return lax.dynamic_index_in_dim(total, (me + d) % 4, 0, keepdims=False)

    a = lax.ppermute(block(1), "dp", shifts[1])
    b = lax.ppermute(block(3), "dp", shifts[-1])
    c = lax.ppermute(block(2), "dp", shifts[2])
    return block(0).astype(F32) + a.astype(F32) + b.astype(F32) + c.astype(F32)


def adam_kernel(slots, grad, w, m, v, w0, w1, c0, c1, master_out, hw, hf, hs):
    new_master, _, _ = adam_update(grad[0], w[...], m[...], v[...])
    master_out[...] = new_master
    for s, (wr, cr) in enumerate(((w0, c0), (w1, c1))):
        m_s, v_s = decode_moments(cr[0])
        nw, nf, ns = adam_update(grad[1 + s], wr[0], m_s, v_s)
        hw[s] = nw.astype(jnp.bfloat16)
        hf[s] = nf
        hs[s] = ns


def finish(slots, grads, w, m, v, all_w, all_codes):
    rows, cols = w.shape
    step = 32

    def plain(i, slots):
        return (i, 0)

    def lead(i, slots):
        return (0, i, 0)

    def held(s):
        return pl.BlockSpec((1, step, cols), lambda i, slots: (slots[s], i, 0))

    flat = pl.BlockSpec((step, cols), plain)
    pair = pl.BlockSpec((2, step, cols), lead)
    return pl.pallas_call(
        adam_kernel,
        grid_spec=pltpu.PrefetchScalarGridSpec(
            num_scalar_prefetch=1,
            grid=(rows // step,),
            in_specs=[pl.BlockSpec((3, step, cols), lead), flat, flat, flat]
            + [held(0), held(1), held(0), held(1)],
            out_specs=[flat, pair, pair, pair],
        ),
        out_shape=[
            jax.ShapeDtypeStruct((rows, cols), F32),
            jax.ShapeDtypeStruct((2, rows, cols), jnp.bfloat16),
            jax.ShapeDtypeStruct((2, rows, cols), F32),
            jax.ShapeDtypeStruct((2, rows, cols), F32),
        ],
        compiler_params=pltpu.CompilerParams(vmem_limit_bytes=32 << 20),
        cost_estimate=pl.CostEstimate(
            flops=60 * rows * cols, bytes_accessed=60 * rows * cols, transcendentals=6 * rows * cols
        ),
    )(slots, grads, w, m, v, all_w, all_w, all_codes, all_codes)


def body(
    saved_inputs,
    saved_cotangents,
    row_counts,
    old_slots,
    new_slots,
    master,
    first_moment,
    second_moment,
):
    expert_index = lax.axis_index("expert")
    data_index = lax.axis_index("dp")
    y, z = data_index // NZ, data_index % NZ
    x, core = expert_index // 2, expert_index % 2
    inputs = saved_inputs[0]
    cot = saved_cotangents[0]
    rows, width_d = inputs.shape
    width_h = cot.shape[1]
    half_h = width_h // 2
    shard = master.shape[1]
    block = width_d // NY
    contract = (((0,), (0,)), ((), ()))
    ys = {d: y_shift(d) for d in (1, 2, -1)}
    zs = {d: z_shift(d) for d in (1, 2, -1)}

    offsets = jnp.array([0, 3, 1, 2], jnp.int32)
    ids = old_slots.reshape(NX, 2, 2)[(x + offsets) % NX]
    ids = jnp.where(core == 0, ids, ids[:, ::-1]).transpose(1, 0, 2).reshape(16)
    mine_new = lax.dynamic_index_in_dim(new_slots, expert_index, 0, keepdims=False)
    targets = jnp.concatenate([expert_index[None].astype(jnp.int32), mine_new])
    table = jnp.where(ids[:, None] == targets[None, :], 0.125, 0.0).astype(F32)

    counts = lax.dynamic_index_in_dim(row_counts[0], data_index, 0, keepdims=False)
    c0, c1 = counts[0], counts[1]
    half = rows // 2

    def scaled(cs, lo, hi):
        index = lax.broadcasted_iota(jnp.int32, (cs.shape[0], 1), 0)
        return jnp.where((index >= lo) & (index < hi), cs * jnp.bfloat16(SCALE), jnp.bfloat16(0))

    def dot(xs, cs):
        return lax.dot_general(xs, cs, contract, preferred_element_type=F32).astype(F16)

    cot0 = scaled(cot[:half], 0, c0)
    a_pieces = {}
    for d in (2, 1, 3, 0):
        xs = lax.dynamic_slice(inputs, (0, ((y + d) % NY) * block), (half, block))
        a_pieces[d] = [
            dot(xs, cot0[:, h * half_h : (h + 1) * half_h]).reshape(NZ, shard, half_h) for h in (0, 1)
        ]
    start = jnp.minimum((c0 // 16) * 16, rows - WINDOW)
    window = lax.dynamic_slice_in_dim(inputs, start, WINDOW, 0)
    cot1 = scaled(lax.dynamic_slice_in_dim(cot, start, WINDOW, 0), c0 - start, c0 + c1 - start)
    b_all = [
        dot(window, cot1[:, h * half_h : (h + 1) * half_h]).reshape(NY, NZ, shard, half_h)
        for h in (0, 1)
    ]
    b_pieces = {
        d: [lax.dynamic_index_in_dim(b, (z + d) % NZ, 1, keepdims=False) for b in b_all]
        for d in (2, 1, 3, 0)
    }

    all_master = lax.all_gather(master[0], "expert", axis=0, tiled=False)
    all_codes = lax.all_gather(
        encode_moments(first_moment[0], second_moment[0]), "expert", axis=0, tiled=False
    )

    sum_a = ring_sums(a_pieces, ys)
    sum_b = ring_sums(b_pieces, zs)
    grad_a = last_sums(sum_a, z, zs)
    grad_b = last_sums(sum_b, y, ys)

    back = 8.0 * 2.0 / SCALE
    mine = [(grad_a * back).astype(F16), (grad_b * back).astype(F16)]
    left = [lax.ppermute(v, "expert", x_shift(1)) for v in mine]
    right = [lax.ppermute(v, "expert", x_shift(-1)) for v in mine]
    far = [lax.ppermute(left[0], "expert", x_shift(1)), lax.ppermute(right[1], "expert", x_shift(-1))]
    same = mine + left + right + far
    other = [lax.ppermute(v, "expert", core_swap()) for v in same]

    grads = 0.0
    for k, g in enumerate(same + other):
        grads = grads + table[k][:, None, None] * g.astype(F32)[None]
    new_master, held_w, held_first, held_second = finish(
        mine_new, grads, master[0], first_moment[0], second_moment[0], all_master, all_codes
    )
    return new_master[None], held_w, held_first, held_second


def solution(mesh):
    return jax.shard_map(
        body,
        mesh=mesh,
        in_specs=(
            P("expert", "dp", None),
            P("expert", "dp", None),
            P("expert", None, None),
            P(),
            P(),
            P("expert", "dp", None),
            P("expert", "dp", None),
            P("expert", "dp", None),
        ),
        out_specs=(
            P("expert", "dp", None),
            P("expert", "dp", None),
            P("expert", "dp", None),
            P("expert", "dp", None),
        ),
        check_vma=False,
    )
```

```python
import functools

import jax
import jax.numpy as jnp
from jax import lax
from jax.experimental import pallas as pl
from jax.experimental.pallas import tpu as pltpu
from jax.sharding import PartitionSpec as P

F16 = jnp.float16
F32 = jnp.float32
NY, NZ, NX = 4, 4, 4
WINDOW = 656
CHUNKS = ((0, 176), (176, 160), (336, 160), (496, 160))
SCALE = 64.0


def plane_shift(d, first):
    pairs = []
    for e in range(2 * NX):
        along_y = (e % 2 == 0) == first
        for j in range(NY * NZ):
            y, z = j // NZ, j % NZ
            to = ((y + d) % NY) * NZ + z if along_y else y * NZ + (z + d) % NZ
            pairs.append((e * NY * NZ + j, e * NY * NZ + to))
    return pairs


def send(value, d, first):
    return lax.ppermute(value, ("expert", "dp"), plane_shift(d, first))


def x_shift(d):
    return [(e, ((e // 2 + d) % NX) * 2 + e % 2) for e in range(2 * NX)]


def send_x(value):
    pairs = [(e, ((e // 2 + (1 if e % 2 == 0 else -1)) % NX) * 2 + e % 2) for e in range(2 * NX)]
    return lax.ppermute(value, "expert", pairs)


def core_swap():
    return [(e, e ^ 1) for e in range(2 * NX)]


def encode_state(w, m, v):
    root = jnp.sqrt(jnp.sqrt(jnp.sqrt(jnp.minimum(jnp.abs(m) * (1.0 / 0.75), 1.0))))
    qm = jnp.round(jnp.where(m < 0, -root, root) * 32767.0).astype(jnp.int32)
    qv = jnp.round(jnp.sqrt(jnp.clip(v * 5.0, 0.0, 1.0)) * 65535.0).astype(jnp.int32)
    return jnp.stack([(w * 2.0**32).astype(jnp.int32), qm * 65536 + qv])


def decode_moments(code):
    qm = lax.shift_right_arithmetic(code, jnp.int32(16)).astype(F32) * (1.0 / 32767.0)
    qv = (code & jnp.int32(0xFFFF)).astype(F32) * (1.0 / 65535.0)
    m2 = qm * qm
    m4 = m2 * m2
    m8 = m4 * m4 * 0.75
    return jnp.where(qm < 0, -m8, m8), qv * qv * 0.2


def partial_kernel(which, here, counts, x, c, *refs):
    outs, (rows, plain, masked, total, load_sems, cot_sem, sems) = refs[:4], refs[4:]
    step = pl.program_id(0)
    core, y, z = here[0], here[1], here[2]
    first, second = counts[y * NZ + z, 0], counts[y * NZ + z, 1]
    if which == 0:
        start, low, high = 0, 0, first
    else:
        start = pl.multiple_of(jnp.minimum(first // 16 * 16, x.shape[0] - WINDOW), 16)
        low, high = first - start, first + second - start
    shard = total.shape[2]
    width = rows.shape[2]
    slot = lax.rem(step, 2)

    def loads(i):
        column = pl.multiple_of(lax.rem(y + 2 + i, NY) * width, width)
        for k, (at, size) in enumerate(CHUNKS):
            yield pltpu.make_async_copy(
                x.at[pl.ds(start + at, size), pl.ds(column, width)],
                rows.at[i, pl.ds(at, size)],
                load_sems.at[i, k],
            )

    @pl.when(step == 0)
    def _():
        cot_load = pltpu.make_async_copy(c.at[pl.ds(start, WINDOW)], plain, cot_sem)
        cot_load.start()
        for i in range(NY):
            for copy in loads(i):
                copy.start()
        cot_load.wait()
        index = lax.broadcasted_iota(jnp.int32, masked.shape, 0)
        value = plain[...].astype(F32) * SCALE
        masked[...] = jnp.where((index >= low) & (index < high), value, 0.0).astype(jnp.bfloat16)

    for copy in loads(step):
        copy.wait()
    product = lax.dot_general(
        rows[step], masked[...], (((0,), (0,)), ((), ())), preferred_element_type=F32
    )

    def wait(slot):
        for b in range(NZ):
            pltpu.make_async_copy(total.at[slot, b], outs[0].at[b], sems.at[slot, b]).wait()

    @pl.when(step >= 2)
    def _():
        wait(slot)

    block = lax.rem(y + 2 + step, NY)
    for b in range(NZ):
        total[slot, b] = product[b * shard : (b + 1) * shard]
        far = jnp.where(core == 0, lax.rem(2 + step, NY), lax.rem(b - z + NZ, NZ))
        place = jnp.where(core == 0, b, block)
        for d in range(4):

            @pl.when(far == d)
            def _():
                pltpu.make_async_copy(
                    total.at[slot, b], outs[d].at[place], sems.at[slot, b]
                ).start()

    @pl.when(step == NY - 1)
    def _():
        wait(1 - slot)
        wait(slot)


def partial(which, here, counts, inputs, cot, shard):
    rows, width_d = inputs.shape
    width_h = cot.shape[1]
    block = width_d // NY
    return pl.pallas_call(
        functools.partial(partial_kernel, which),
        grid_spec=pltpu.PrefetchScalarGridSpec(
            num_scalar_prefetch=2,
            grid=(NY,),
            in_specs=[
                pl.BlockSpec(memory_space=pl.ANY),
                pl.BlockSpec(memory_space=pl.ANY),
            ],
            out_specs=[pl.BlockSpec(memory_space=pltpu.HBM)] * 4,
            scratch_shapes=[
                pltpu.VMEM((NY, WINDOW, block), jnp.bfloat16),
                pltpu.VMEM((WINDOW, width_h), jnp.bfloat16),
                pltpu.VMEM((WINDOW, width_h), jnp.bfloat16),
                pltpu.VMEM((2, NZ, shard, width_h), F32),
                pltpu.SemaphoreType.DMA((NY, len(CHUNKS))),
                pltpu.SemaphoreType.DMA,
                pltpu.SemaphoreType.DMA((2, NZ)),
            ],
        ),
        out_shape=[pltpu.HBM((4, shard, width_h), F32)] * 4,
        compiler_params=pltpu.CompilerParams(vmem_limit_bytes=20 << 20),
        cost_estimate=pl.CostEstimate(
            flops=2 * WINDOW * width_d * width_h * 4, bytes_accessed=rows * width_d * 8, transcendentals=0
        ),
    )(here, counts, inputs, cot)


def exchange(total, me):
    def block(d):
        return lax.dynamic_index_in_dim(total, (me + d) % 4, 0, keepdims=False)

    return [block(0), send(block(1), 1, False), send(block(3), -1, False), send(block(2), 2, False)]


def add_up(parts):
    return sum(p.astype(F32) for p in parts)


def prepare_kernel(pick, *refs):
    sources = [ref.at[i] for ref in refs[:3] for i in range(2)] + list(refs[3:5])
    held, state, sems = refs[5:]
    for s in range(2):
        for k in range(8):

            @pl.when(pick[s] == k)
            def _():
                pltpu.make_async_copy(sources[k], state.at[s], sems.at[s]).start()

    for s in range(2):
        pltpu.make_async_copy(sources[0], state.at[s], sems.at[s]).wait()

        @pl.loop(0, state.shape[2], step=32)
        def _(at):
            part = pl.ds(pl.multiple_of(at, 32), 32)
            m, v = decode_moments(state[s, 1, part])
            held[0, s, part] = state[s, 0, part].astype(F32) * 2.0**-32
            held[1, s, part] = 0.9 * m
            held[2, s, part] = 0.95 * v


def prepare(pick, pairs, singles):
    _, rows, cols = singles[0].shape
    sources = pairs + singles
    sources = [pltpu.with_memory_space_constraint(v, pltpu.HBM) for v in sources]
    return pl.pallas_call(
        prepare_kernel,
        grid_spec=pltpu.PrefetchScalarGridSpec(
            num_scalar_prefetch=1,
            grid=(1,),
            in_specs=[pl.BlockSpec(memory_space=pl.ANY)] * 5,
            out_specs=pl.BlockSpec((3, 2, rows, cols), lambda i, pick: (0, 0, 0, 0)),
            scratch_shapes=[
                pltpu.VMEM((2, 2, rows, cols), jnp.int32),
                pltpu.SemaphoreType.DMA((2,)),
            ],
        ),
        out_shape=jax.ShapeDtypeStruct((3, 2, rows, cols), F32),
        compiler_params=pltpu.CompilerParams(vmem_limit_bytes=16 << 20),
    )(pick, *sources)


def adam_tail(gradient, w, m_decayed, v_decayed):
    first_new = m_decayed + 0.1 * gradient
    second_new = v_decayed + 0.05 * gradient * gradient
    root = jnp.sqrt(second_new * (1.0 / (1.0 - 0.95**20))) + 1e-08
    corrected = first_new * (1.0 / (1.0 - 0.9**20)) / root
    return w - 0.001 * (corrected + 0.1 * w), first_new, second_new


def adam_kernel(grad, w, m, v, held, master_out, hw, hf, hs):
    master_out[...] = adam_tail(grad[0], w[...], 0.9 * m[...], 0.95 * v[...])[0]
    for s in range(2):
        nw, nf, ns = adam_tail(grad[1 + s], held[0, s], held[1, s], held[2, s])
        hw[s] = nw.astype(jnp.bfloat16)
        hf[s] = nf
        hs[s] = ns


def finish(grads, w, m, v, held):
    rows, cols = w.shape
    step = 32
    flat = pl.BlockSpec((step, cols), lambda i: (i, 0))
    pair = pl.BlockSpec((2, step, cols), lambda i: (0, i, 0))
    return pl.pallas_call(
        adam_kernel,
        grid=(rows // step,),
        in_specs=[pl.BlockSpec((3, step, cols), lambda i: (0, i, 0)), flat, flat, flat]
        + [pl.BlockSpec((3, 2, step, cols), lambda i: (0, 0, i, 0))],
        out_specs=[flat, pair, pair, pair],
        out_shape=[
            jax.ShapeDtypeStruct((rows, cols), F32),
            jax.ShapeDtypeStruct((2, rows, cols), jnp.bfloat16),
            jax.ShapeDtypeStruct((2, rows, cols), F32),
            jax.ShapeDtypeStruct((2, rows, cols), F32),
        ],
        compiler_params=pltpu.CompilerParams(vmem_limit_bytes=10 << 20),
    )(grads, w, m, v, held)


def body(
    saved_inputs,
    saved_cotangents,
    row_counts,
    old_slots,
    new_slots,
    master,
    first_moment,
    second_moment,
):
    expert_index = lax.axis_index("expert")
    data_index = lax.axis_index("dp")
    y, z = data_index // NZ, data_index % NZ
    x, core = expert_index // 2, expert_index % 2
    inputs = saved_inputs[0]
    cot = saved_cotangents[0]
    rows = inputs.shape[0]
    shard = master.shape[1]
    offsets = jnp.array([0, 3, 1, 2], jnp.int32)
    ids = old_slots.reshape(NX, 2, 2)[(x + offsets) % NX]
    ids = jnp.where(core == 0, ids, ids[:, ::-1]).transpose(1, 0, 2).reshape(16)
    mine_new = lax.dynamic_index_in_dim(new_slots, expert_index, 0, keepdims=False)
    targets = jnp.concatenate([expert_index[None].astype(jnp.int32), mine_new])
    table = jnp.where(ids[:, None] == targets[None, :], 0.125, 0.0).astype(F32)

    here = jnp.stack([core, y, z])
    inputs = pltpu.with_memory_space_constraint(inputs, pltpu.HBM)
    cot = pltpu.with_memory_space_constraint(cot, pltpu.HBM)
    part0 = partial(0, here, row_counts[0], inputs, cot, shard)
    far_up = send(part0[2].astype(F16), 1, True)
    raw_down = send(part0[3].astype(F16), -1, True)
    w_late, m_late, v_late, part0 = lax.optimization_barrier(
        (master[0], first_moment[0], second_moment[0], part0)
    )
    state = encode_state(w_late, m_late, v_late)
    pair = jnp.stack([state, lax.ppermute(state, "expert", core_swap())])
    beside = send_x(pair)
    far_state = send_x(beside[0])
    pairs = [pair, beside, lax.ppermute(beside, "expert", core_swap())]
    singles = [far_state, lax.ppermute(far_state, "expert", core_swap())]
    cot, state = lax.optimization_barrier((cot, state))
    part1 = partial(1, here, row_counts[0], inputs, cot, shard)
    part1, far_up, raw_down = lax.optimization_barrier((part1, far_up, raw_down))
    far_down = send(part1[2].astype(F16), -1, True)
    raw_up = send(part1[1].astype(F16), 1, True)

    far_down, raw_up = lax.optimization_barrier((far_down, raw_up))
    both_up = send((part0[1] + far_up.astype(F32)).astype(F16), 1, True)
    both_down = send((part1[3] + far_down.astype(F32)).astype(F16), -1, True)
    sum_a = (part0[0] + both_up.astype(F32) + raw_down.astype(F32)) * 0.5
    sum_b = (part1[0] + raw_up.astype(F32) + both_down.astype(F32)) * 0.5
    me = jnp.where(core == 0, z, y)
    parts_a = exchange(sum_a.astype(F16), me)
    parts_b = exchange(sum_b.astype(F16), me)
    parts_a, parts_b[1] = lax.optimization_barrier((parts_a, parts_b[1]))

    back = 8.0 * 2.0 / SCALE

    def spread(parts):
        own = (add_up(parts) * back).astype(F16)
        return [own] + [lax.ppermute(own, "expert", x_shift(d)) for d in (1, -1, 2)]

    same_a = spread(parts_a)
    same_b = spread(parts_b)
    same_a, same_b[0] = lax.optimization_barrier((same_a, same_b[0]))
    other_a = [lax.ppermute(v, "expert", core_swap()) for v in same_a]
    other_a, pairs, singles, same_b[1] = lax.optimization_barrier(
        (other_a, pairs, singles, same_b[1])
    )

    def weighted(same, other, s):
        total = 0.0
        for k, g in enumerate(same + other):
            total = total + table[2 * k + s][:, None, None] * g.astype(F32)[None]
        return total

    at = (mine_new // 2 - x) % NX
    twist = (mine_new % 2 != core).astype(jnp.int32)
    near = jnp.where((at == 3) == (core == 0), 2 + twist, 5 - twist)
    pick = jnp.where(at == 0, twist, jnp.where(at == 2, 6 + twist, near))
    held = prepare(pick, pairs, singles)
    grads_a = weighted(same_a, other_a, 0)
    same_b[2], same_b[3], held, grads_a = lax.optimization_barrier(
        (same_b[2], same_b[3], held, grads_a)
    )
    other_b = [lax.ppermute(v, "expert", core_swap()) for v in same_b]
    grads = grads_a + weighted(same_b, other_b, 1)
    new_master, held_w, held_first, held_second = finish(
        grads, master[0], first_moment[0], second_moment[0], held
    )
    return new_master[None], held_w, held_first, held_second


def solution(mesh):
    return jax.shard_map(
        body,
        mesh=mesh,
        in_specs=(
            P("expert", "dp", None),
            P("expert", "dp", None),
            P("expert", None, None),
            P(),
            P(),
            P("expert", "dp", None),
            P("expert", "dp", None),
            P("expert", "dp", None),
        ),
        out_specs=(
            P("expert", "dp", None),
            P("expert", "dp", None),
            P("expert", "dp", None),
            P("expert", "dp", None),
        ),
        check_vma=False,
    )
```

```python
import functools

import jax
import jax.numpy as jnp
from jax import lax
from jax.experimental import pallas as pl
from jax.experimental.pallas import tpu as pltpu
from jax.sharding import PartitionSpec as P

F16 = jnp.float16
F32 = jnp.float32
NY, NZ, NX = 4, 4, 4
WINDOW = 656
CHUNKS = ((0, 176), (176, 160), (336, 160), (496, 160))
SCALE = 64.0


def plane_shift(d, first):
    pairs = []
    for e in range(2 * NX):
        along_y = (e % 2 == 0) == first
        for j in range(NY * NZ):
            y, z = j // NZ, j % NZ
            to = ((y + d) % NY) * NZ + z if along_y else y * NZ + (z + d) % NZ
            pairs.append((e * NY * NZ + j, e * NY * NZ + to))
    return pairs


def send(value, d, first):
    return lax.ppermute(value, ("expert", "dp"), plane_shift(d, first))


def x_shift(d):
    return [(e, ((e // 2 + d) % NX) * 2 + e % 2) for e in range(2 * NX)]


def send_x(value):
    pairs = [(e, ((e // 2 + (1 if e % 2 == 0 else -1)) % NX) * 2 + e % 2) for e in range(2 * NX)]
    return lax.ppermute(value, "expert", pairs)


def core_swap():
    return [(e, e ^ 1) for e in range(2 * NX)]


def encode_state(w, m, v):
    root = jnp.sqrt(jnp.sqrt(jnp.sqrt(jnp.minimum(jnp.abs(m) * (1.0 / 0.75), 1.0))))
    qm = jnp.round(jnp.where(m < 0, -root, root) * 32767.0).astype(jnp.int32)
    qv = jnp.round(jnp.sqrt(jnp.clip(v * 5.0, 0.0, 1.0)) * 65535.0).astype(jnp.int32)
    return (w * 2.0**32).astype(jnp.int32), qm * 65536 + qv


def decode_moments(code):
    qm = lax.shift_right_arithmetic(code, jnp.int32(16)).astype(F32) * (1.0 / 32767.0)
    qv = (code & jnp.int32(0xFFFF)).astype(F32) * (1.0 / 65535.0)
    m2 = qm * qm
    m4 = m2 * m2
    m8 = m4 * m4 * 0.75
    return jnp.where(qm < 0, -m8, m8), qv * qv * 0.2


def partial_kernel(which, here, counts, x, c, *refs):
    if which == 0:
        owned, outs, state_out, refs = refs[:3], refs[3:7], refs[7], refs[8:]
        held, state, held_sems, state_sem = refs[7:]
    else:
        outs, refs = refs[:4], refs[4:]
    rows, plain, masked, total, load_sems, cot_sem, sems = refs[:7]
    step = pl.program_id(0)
    core, y, z = here[0], here[1], here[2]
    first, second = counts[y * NZ + z, 0], counts[y * NZ + z, 1]
    if which == 0:
        start, low, high = 0, 0, first
    else:
        start = pl.multiple_of(jnp.minimum(first // 16 * 16, x.shape[0] - WINDOW), 16)
        low, high = first - start, first + second - start
    shard = total.shape[2]
    width = rows.shape[2]
    slot = lax.rem(step, 2)

    def loads(i):
        column = pl.multiple_of(lax.rem(y + 2 + i, NY) * width, width)
        for k, (at, size) in enumerate(CHUNKS):
            yield pltpu.make_async_copy(
                x.at[pl.ds(start + at, size), pl.ds(column, width)],
                rows.at[i, pl.ds(at, size)],
                load_sems.at[i, k],
            )

    @pl.when(step == 0)
    def _():
        cot_load = pltpu.make_async_copy(c.at[pl.ds(start, WINDOW)], plain, cot_sem)
        cot_load.start()
        for copy in loads(0):
            copy.start()
        cot_load.wait()
        index = lax.broadcasted_iota(jnp.int32, masked.shape, 0)
        value = plain[...].astype(F32) * SCALE
        masked[...] = jnp.where((index >= low) & (index < high), value, 0.0).astype(jnp.bfloat16)
        for i in range(1, NY):
            for copy in loads(i):
                copy.start()
        if which == 0:
            for k in range(3):
                pltpu.make_async_copy(owned[k], held.at[k], held_sems.at[k]).start()

    if which == 0:

        @pl.when(step == 2)
        def _():
            for k in range(3):
                pltpu.make_async_copy(owned[k], held.at[k], held_sems.at[k]).wait()

            @pl.loop(0, shard, step=32)
            def _(at):
                part = pl.ds(pl.multiple_of(at, 32), 32)
                state[0, part], state[1, part] = encode_state(
                    held[0, part], held[1, part], held[2, part]
                )

            pltpu.make_async_copy(state, state_out, state_sem).start()

        @pl.when(step == NY - 1)
        def _():
            pltpu.make_async_copy(state, state_out, state_sem).wait()

    for copy in loads(step):
        copy.wait()

    def wait(slot):
        pltpu.make_async_copy(total.at[slot], outs[0], sems.at[slot]).wait()

    @pl.when(step >= 2)
    def _():
        wait(slot)

    product = lax.dot_general(
        rows[step], masked[...], (((0,), (0,)), ((), ())), preferred_element_type=F32
    )
    for b in range(NZ):
        total[slot, b] = product[b * shard : (b + 1) * shard]

    for d in range(4):

        @pl.when((core == 0) & (lax.rem(2 + step, NY) == d))
        def _():
            pltpu.make_async_copy(total.at[slot], outs[d], sems.at[slot]).start()

        @pl.when((core == 1) & (z == d))
        def _():
            for b in range(NZ):
                pltpu.make_async_copy(
                    total.at[slot, b], outs[(b - d) % NZ].at[lax.rem(y + 2 + step, NY)], sems.at[slot]
                ).start()

    @pl.when(step == NY - 1)
    def _():
        wait(1 - slot)
        wait(slot)


def partial(which, here, counts, inputs, cot, shard, owned=()):
    rows, width_d = inputs.shape
    width_h = cot.shape[1]
    block = width_d // NY
    piece = pltpu.HBM((4, shard, width_h), F32)
    out_shape = [piece] * 4
    scratch = [
        pltpu.VMEM((NY, WINDOW, block), jnp.bfloat16),
        pltpu.VMEM((WINDOW, width_h), jnp.bfloat16),
        pltpu.VMEM((WINDOW, width_h), jnp.bfloat16),
        pltpu.VMEM((2, NZ, shard, width_h), F32),
        pltpu.SemaphoreType.DMA((NY, len(CHUNKS))),
        pltpu.SemaphoreType.DMA,
        pltpu.SemaphoreType.DMA((2,)),
    ]
    if which == 0:
        out_shape = out_shape + [pltpu.HBM((2, shard, width_h), jnp.int32)]
        scratch = scratch + [
            pltpu.VMEM((3, shard, width_h), F32),
            pltpu.VMEM((2, shard, width_h), jnp.int32),
            pltpu.SemaphoreType.DMA((3,)),
            pltpu.SemaphoreType.DMA,
        ]
    operands = [pltpu.with_memory_space_constraint(v, pltpu.HBM) for v in (inputs, cot, *owned)]
    return pl.pallas_call(
        functools.partial(partial_kernel, which),
        grid_spec=pltpu.PrefetchScalarGridSpec(
            num_scalar_prefetch=2,
            grid=(NY,),
            in_specs=[pl.BlockSpec(memory_space=pl.ANY)] * len(operands),
            out_specs=[pl.BlockSpec(memory_space=pltpu.HBM)] * len(out_shape),
            scratch_shapes=scratch,
        ),
        out_shape=out_shape,
        compiler_params=pltpu.CompilerParams(vmem_limit_bytes=28 << 20),
        cost_estimate=pl.CostEstimate(flops=1 << 33, bytes_accessed=1 << 24, transcendentals=0),
    )(here, counts, *operands)


def exchange(total):
    groups = []
    for e in range(2 * NX):
        for fixed in range(4):
            members = [fixed * NZ + q if e % 2 == 0 else q * NZ + fixed for q in range(4)]
            groups.append([e * NY * NZ + j for j in members])
    return lax.all_to_all(total, ("expert", "dp"), 0, 0, axis_index_groups=groups, tiled=True)


def add_up(parts):
    return sum(p.astype(F32) for p in parts)


def prepare_kernel(pick, *refs):
    sources = [ref.at[i] for ref in refs[:3] for i in range(2)] + list(refs[3:5])
    held, state, sems = refs[5:]
    for s in range(2):
        for k in range(8):

            @pl.when(pick[s] == k)
            def _():
                pltpu.make_async_copy(sources[k], state.at[s], sems.at[s]).start()

    for s in range(2):
        pltpu.make_async_copy(sources[0], state.at[s], sems.at[s]).wait()

        @pl.loop(0, state.shape[2], step=32)
        def _(at):
            part = pl.ds(pl.multiple_of(at, 32), 32)
            m, v = decode_moments(state[s, 1, part])
            held[0, s, part] = state[s, 0, part].astype(F32) * 2.0**-32
            held[1, s, part] = 0.9 * m
            held[2, s, part] = 0.95 * v


def prepare(pick, pairs, singles):
    _, rows, cols = singles[0].shape
    sources = pairs + singles
    sources = [pltpu.with_memory_space_constraint(v, pltpu.HBM) for v in sources]
    return pl.pallas_call(
        prepare_kernel,
        grid_spec=pltpu.PrefetchScalarGridSpec(
            num_scalar_prefetch=1,
            grid=(1,),
            in_specs=[pl.BlockSpec(memory_space=pl.ANY)] * 5,
            out_specs=pl.BlockSpec((3, 2, rows, cols), lambda i, pick: (0, 0, 0, 0)),
            scratch_shapes=[
                pltpu.VMEM((2, 2, rows, cols), jnp.int32),
                pltpu.SemaphoreType.DMA((2,)),
            ],
        ),
        out_shape=jax.ShapeDtypeStruct((3, 2, rows, cols), F32),
        compiler_params=pltpu.CompilerParams(vmem_limit_bytes=16 << 20),
    )(pick, *sources)


def adam_tail(gradient, w, m_decayed, v_decayed):
    first_new = m_decayed + 0.1 * gradient
    second_new = v_decayed + 0.05 * gradient * gradient
    root = jnp.sqrt(second_new * (1.0 / (1.0 - 0.95**20))) + 1e-08
    corrected = first_new * (1.0 / (1.0 - 0.9**20)) / root
    return w - 0.001 * (corrected + 0.1 * w), first_new, second_new


def adam_kernel(grad_own, grad_0, grad_1, w, m, v, held, master_out, hw, hf, hs):
    master_out[...] = adam_tail(grad_own[...], w[...], 0.9 * m[...], 0.95 * v[...])[0]
    for s, grad in enumerate((grad_0, grad_1)):
        nw, nf, ns = adam_tail(grad[...], held[0, s], held[1, s], held[2, s])
        hw[s] = nw.astype(jnp.bfloat16)
        hf[s] = nf
        hs[s] = ns


def finish(grads, w, m, v, held):
    rows, cols = w.shape
    step = 32
    flat = pl.BlockSpec((step, cols), lambda i: (i, 0))
    pair = pl.BlockSpec((2, step, cols), lambda i: (0, i, 0))
    return pl.pallas_call(
        adam_kernel,
        grid=(rows // step,),
        in_specs=[flat] * 6
        + [pl.BlockSpec((3, 2, step, cols), lambda i: (0, 0, i, 0))],
        out_specs=[flat, pair, pair, pair],
        out_shape=[
            jax.ShapeDtypeStruct((rows, cols), F32),
            jax.ShapeDtypeStruct((2, rows, cols), jnp.bfloat16),
            jax.ShapeDtypeStruct((2, rows, cols), F32),
            jax.ShapeDtypeStruct((2, rows, cols), F32),
        ],
        compiler_params=pltpu.CompilerParams(vmem_limit_bytes=10 << 20),
    )(*grads, w, m, v, held)


def body(
    saved_inputs,
    saved_cotangents,
    row_counts,
    old_slots,
    new_slots,
    master,
    first_moment,
    second_moment,
):
    expert_index = lax.axis_index("expert")
    data_index = lax.axis_index("dp")
    y, z = data_index // NZ, data_index % NZ
    x, core = expert_index // 2, expert_index % 2
    inputs = saved_inputs[0]
    cot = saved_cotangents[0]
    rows = inputs.shape[0]
    shard = master.shape[1]
    offsets = jnp.array([0, 3, 1, 2], jnp.int32)
    ids = old_slots.reshape(NX, 2, 2)[(x + offsets) % NX]
    ids = jnp.where(core == 0, ids, ids[:, ::-1]).transpose(1, 0, 2).reshape(16)
    mine_new = lax.dynamic_index_in_dim(new_slots, expert_index, 0, keepdims=False)
    targets = jnp.concatenate([expert_index[None].astype(jnp.int32), mine_new])
    table = jnp.where(ids[:, None] == targets[None, :], 0.125, 0.0).astype(F32)
    table = jnp.broadcast_to(table[:, :, None, None], (16, 3, 1, master.shape[2]))
    table = lax.optimization_barrier(table)

    here = jnp.stack([core, y, z])
    *part0, state = partial(
        0, here, row_counts[0], inputs, cot, shard, (master[0], first_moment[0], second_moment[0])
    )
    other_state = lax.ppermute(state, "expert", core_swap())
    small = [part0[2].astype(F16), part0[3].astype(F16)]
    small, other_state = lax.optimization_barrier((small, other_state))
    far_up = send(small[0], 1, True)
    raw_down = send(small[1], -1, True)
    pair = jnp.stack([state, other_state])
    beside = send_x(pair)

    cot, part0, pair = lax.optimization_barrier((cot, part0, pair))
    part1 = partial(1, here, row_counts[0], inputs, cot, shard)
    part1, far_up, raw_down = lax.optimization_barrier((part1, far_up, raw_down))
    far_down = send(part1[2].astype(F16), -1, True)
    both_up = send((part0[1] + far_up.astype(F32)).astype(F16), 1, True)
    far_down, both_up, part1_near = lax.optimization_barrier((far_down, both_up, part1[1]))
    raw_up = send(part1_near.astype(F16), 1, True)
    both_down = send((part1[3] + far_down.astype(F32)).astype(F16), -1, True)
    back = 8.0 * 2.0 / SCALE

    def swap(value):
        return lax.ppermute(value, "expert", core_swap())

    def spread(got):
        own = (jnp.sum(got.astype(F32), 0) * back).astype(F16)
        return [own] + [lax.ppermute(own, "expert", x_shift(d)) for d in (1, -1, 2)]

    beside, both_up = lax.optimization_barrier((beside, both_up))
    far_state = send_x(beside[0])
    cross_state = swap(beside)
    sum_a = (part0[0] + both_up.astype(F32) + raw_down.astype(F32)) * 0.5
    got_a = exchange(sum_a.astype(F16))
    got_a, both_down, raw_up, far_state, cross_state = lax.optimization_barrier(
        (got_a, both_down, raw_up, far_state, cross_state)
    )
    sum_b = (part1[0] + raw_up.astype(F32) + both_down.astype(F32)) * 0.5
    got_b = exchange(sum_b.astype(F16))
    same_a = spread(got_a)

    at = (mine_new // 2 - x) % NX
    twist = (mine_new % 2 != core).astype(jnp.int32)
    near = jnp.where((at == 3) == (core == 0), 2 + twist, 5 - twist)
    pick = jnp.where(at == 0, twist, jnp.where(at == 2, 6 + twist, near))
    held = prepare(pick, [pair, beside, cross_state], [far_state, swap(far_state)])
    got_b, same_a, held = lax.optimization_barrier((got_b, same_a, held))
    same_b = spread(got_b)
    other_a = [swap(v) for v in same_a]
    other_a, same_b = lax.optimization_barrier((other_a, same_b))

    def weighted(same, other, s, t):
        total = 0.0
        for k, g in enumerate(same + other):
            total = total + table[2 * k + s, t] * g.astype(F32)
        return total

    grads_a = [weighted(same_a, other_a, 0, t) for t in range(3)]
    grads_a = lax.optimization_barrier(grads_a)
    other_b = [lax.ppermute(v, "expert", core_swap()) for v in same_b]
    grads = [grads_a[t] + weighted(same_b, other_b, 1, t) for t in range(3)]
    new_master, held_w, held_first, held_second = finish(
        grads, master[0], first_moment[0], second_moment[0], held
    )
    return new_master[None], held_w, held_first, held_second


def solution(mesh):
    return jax.shard_map(
        body,
        mesh=mesh,
        in_specs=(
            P("expert", "dp", None),
            P("expert", "dp", None),
            P("expert", None, None),
            P(),
            P(),
            P("expert", "dp", None),
            P("expert", "dp", None),
            P("expert", "dp", None),
        ),
        out_specs=(
            P("expert", "dp", None),
            P("expert", "dp", None),
            P("expert", "dp", None),
            P("expert", "dp", None),
        ),
        check_vma=False,
    )
```

```python
import functools

import jax
import jax.numpy as jnp
from jax import lax
from jax.experimental import pallas as pl
from jax.experimental.pallas import tpu as pltpu
from jax.sharding import PartitionSpec as P

F16 = jnp.float16
F32 = jnp.float32
NY, NZ, NX = 4, 4, 4
WINDOW = 656
CHUNKS = ((0, 176), (176, 160), (336, 160), (496, 160))
SCALE = 64.0


def plane_shift(d, first):
    pairs = []
    for e in range(2 * NX):
        along_y = (e % 2 == 0) == first
        for j in range(NY * NZ):
            y, z = j // NZ, j % NZ
            to = ((y + d) % NY) * NZ + z if along_y else y * NZ + (z + d) % NZ
            pairs.append((e * NY * NZ + j, e * NY * NZ + to))
    return pairs


def send(value, d, first):
    return lax.ppermute(value, ("expert", "dp"), plane_shift(d, first))


def x_shift(d):
    return [(e, ((e // 2 + d) % NX) * 2 + e % 2) for e in range(2 * NX)]


def send_x(value):
    pairs = [(e, ((e // 2 + (1 if e % 2 == 0 else -1)) % NX) * 2 + e % 2) for e in range(2 * NX)]
    return lax.ppermute(value, "expert", pairs)


def core_swap():
    return [(e, e ^ 1) for e in range(2 * NX)]


def encode_state(w, m, v):
    root = jnp.exp2(0.125 * jnp.log2(jnp.clip(jnp.abs(m) * (1.0 / 0.75), 1e-30, 1.0)))
    qm = jnp.round(jnp.where(m < 0, -root, root) * 32767.0).astype(jnp.int32)
    qv = jnp.round(jnp.sqrt(jnp.clip(v * 5.0, 0.0, 1.0)) * 65535.0).astype(jnp.int32)
    return (w * 2.0**32).astype(jnp.int32), qm * 65536 + qv


def decode_moments(code):
    qm = lax.shift_right_arithmetic(code, jnp.int32(16)).astype(F32) * (1.0 / 32767.0)
    qv = (code & jnp.int32(0xFFFF)).astype(F32) * (1.0 / 65535.0)
    m2 = qm * qm
    m4 = m2 * m2
    m8 = m4 * m4 * 0.75
    return jnp.where(qm < 0, -m8, m8), qv * qv * 0.2


def partial_kernel(which, here, counts, x, c, *refs):
    if which == 0:
        owned, outs, state_out, refs = refs[:3], refs[3:7], refs[7], refs[8:]
        held, state, held_sems, state_sem = refs[7:]
    else:
        outs, refs = refs[:4], refs[4:]
    rows, plain, masked, total, load_sems, cot_sem, sems = refs[:7]
    step = pl.program_id(0)
    core, y, z = here[0], here[1], here[2]
    first, second = counts[y * NZ + z, 0], counts[y * NZ + z, 1]
    if which == 0:
        start, low, high = 0, 0, first
    else:
        start = pl.multiple_of(jnp.minimum(first // 16 * 16, x.shape[0] - WINDOW), 16)
        low, high = first - start, first + second - start
    shard = total.shape[2]
    width = rows.shape[2]
    slot = lax.rem(step, 2)

    def loads(i):
        column = pl.multiple_of(lax.rem(y + 2 + i, NY) * width, width)
        for k, (at, size) in enumerate(CHUNKS):
            yield pltpu.make_async_copy(
                x.at[pl.ds(start + at, size), pl.ds(column, width)],
                rows.at[i, pl.ds(at, size)],
                load_sems.at[i, k],
            )

    @pl.when(step == 0)
    def _():
        cot_load = pltpu.make_async_copy(c.at[pl.ds(start, WINDOW)], plain, cot_sem)
        cot_load.start()
        for copy in loads(0):
            copy.start()
        cot_load.wait()
        index = lax.broadcasted_iota(jnp.int32, masked.shape, 0)
        value = plain[...].astype(F32) * SCALE
        masked[...] = jnp.where((index >= low) & (index < high), value, 0.0).astype(jnp.bfloat16)
        for i in range(1, NY):
            for copy in loads(i):
                copy.start()
        if which == 0:
            for k in range(3):
                pltpu.make_async_copy(owned[k], held.at[k], held_sems.at[k]).start()

    if which == 0:

        @pl.when(step == 2)
        def _():
            for k in range(3):
                pltpu.make_async_copy(owned[k], held.at[k], held_sems.at[k]).wait()

            @pl.loop(0, shard, step=32)
            def _(at):
                part = pl.ds(pl.multiple_of(at, 32), 32)
                state[0, part], state[1, part] = encode_state(
                    held[0, part], held[1, part], held[2, part]
                )

            pltpu.make_async_copy(state, state_out, state_sem).start()

        @pl.when(step == NY - 1)
        def _():
            pltpu.make_async_copy(state, state_out, state_sem).wait()

    for copy in loads(step):
        copy.wait()

    def wait(slot):
        pltpu.make_async_copy(total.at[slot], outs[0], sems.at[slot]).wait()

    @pl.when(step >= 2)
    def _():
        wait(slot)

    product = lax.dot_general(
        rows[step], masked[...], (((0,), (0,)), ((), ())), preferred_element_type=F32
    )
    for b in range(NZ):
        total[slot, b] = product[b * shard : (b + 1) * shard]

    for d in range(4):

        @pl.when((core == 0) & (lax.rem(2 + step, NY) == d))
        def _():
            pltpu.make_async_copy(total.at[slot], outs[d], sems.at[slot]).start()

        @pl.when((core == 1) & (z == d))
        def _():
            for b in range(NZ):
                pltpu.make_async_copy(
                    total.at[slot, b], outs[(b - d) % NZ].at[lax.rem(y + 2 + step, NY)], sems.at[slot]
                ).start()

    @pl.when(step == NY - 1)
    def _():
        wait(1 - slot)
        wait(slot)


def partial(which, here, counts, inputs, cot, shard, owned=()):
    rows, width_d = inputs.shape
    width_h = cot.shape[1]
    block = width_d // NY
    piece = pltpu.HBM((4, shard, width_h), F32)
    out_shape = [piece] * 4
    scratch = [
        pltpu.VMEM((NY, WINDOW, block), jnp.bfloat16),
        pltpu.VMEM((WINDOW, width_h), jnp.bfloat16),
        pltpu.VMEM((WINDOW, width_h), jnp.bfloat16),
        pltpu.VMEM((2, NZ, shard, width_h), F32),
        pltpu.SemaphoreType.DMA((NY, len(CHUNKS))),
        pltpu.SemaphoreType.DMA,
        pltpu.SemaphoreType.DMA((2,)),
    ]
    if which == 0:
        out_shape = out_shape + [pltpu.HBM((2, shard, width_h), jnp.int32)]
        scratch = scratch + [
            pltpu.VMEM((3, shard, width_h), F32),
            pltpu.VMEM((2, shard, width_h), jnp.int32),
            pltpu.SemaphoreType.DMA((3,)),
            pltpu.SemaphoreType.DMA,
        ]
    operands = [pltpu.with_memory_space_constraint(v, pltpu.HBM) for v in (inputs, cot, *owned)]
    return pl.pallas_call(
        functools.partial(partial_kernel, which),
        grid_spec=pltpu.PrefetchScalarGridSpec(
            num_scalar_prefetch=2,
            grid=(NY,),
            in_specs=[pl.BlockSpec(memory_space=pl.ANY)] * len(operands),
            out_specs=[pl.BlockSpec(memory_space=pltpu.HBM)] * len(out_shape),
            scratch_shapes=scratch,
        ),
        out_shape=out_shape,
        compiler_params=pltpu.CompilerParams(vmem_limit_bytes=28 << 20),
        cost_estimate=pl.CostEstimate(flops=1 << 33, bytes_accessed=1 << 24, transcendentals=0),
    )(here, counts, *operands)


def exchange(total):
    groups = []
    for e in range(2 * NX):
        for fixed in range(4):
            members = [fixed * NZ + q if e % 2 == 0 else q * NZ + fixed for q in range(4)]
            groups.append([e * NY * NZ + j for j in members])
    return lax.all_to_all(total, ("expert", "dp"), 0, 0, axis_index_groups=groups, tiled=True)


def add_up(parts):
    return sum(p.astype(F32) for p in parts)


def prepare_kernel(pick, *refs):
    sources = [ref.at[i] for ref in refs[:3] for i in range(2)] + list(refs[3:5])
    held, state, sems = refs[5:]
    for s in range(2):
        for k in range(8):

            @pl.when(pick[s] == k)
            def _():
                pltpu.make_async_copy(sources[k], state.at[s], sems.at[s]).start()

    for s in range(2):
        pltpu.make_async_copy(sources[0], state.at[s], sems.at[s]).wait()

        @pl.loop(0, state.shape[2], step=32)
        def _(at):
            part = pl.ds(pl.multiple_of(at, 32), 32)
            m, v = decode_moments(state[s, 1, part])
            held[0, s, part] = state[s, 0, part].astype(F32) * 2.0**-32
            held[1, s, part] = 0.9 * m
            held[2, s, part] = 0.95 * v


def prepare(pick, pairs, singles):
    _, rows, cols = singles[0].shape
    sources = pairs + singles
    sources = [pltpu.with_memory_space_constraint(v, pltpu.HBM) for v in sources]
    return pl.pallas_call(
        prepare_kernel,
        grid_spec=pltpu.PrefetchScalarGridSpec(
            num_scalar_prefetch=1,
            grid=(1,),
            in_specs=[pl.BlockSpec(memory_space=pl.ANY)] * 5,
            out_specs=pl.BlockSpec((3, 2, rows, cols), lambda i, pick: (0, 0, 0, 0)),
            scratch_shapes=[
                pltpu.VMEM((2, 2, rows, cols), jnp.int32),
                pltpu.SemaphoreType.DMA((2,)),
            ],
        ),
        out_shape=jax.ShapeDtypeStruct((3, 2, rows, cols), F32),
        compiler_params=pltpu.CompilerParams(vmem_limit_bytes=16 << 20),
    )(pick, *sources)


def adam_tail(gradient, w, m_decayed, v_decayed):
    first_new = m_decayed + 0.1 * gradient
    second_new = v_decayed + 0.05 * gradient * gradient
    root = jnp.sqrt(second_new * (1.0 / (1.0 - 0.95**20))) + 1e-08
    corrected = first_new * (1.0 / (1.0 - 0.9**20)) / root
    return w - 0.001 * (corrected + 0.1 * w), first_new, second_new


def adam_kernel(grad_own, grad_0, grad_1, w, m, v, held, master_out, hw, hf, hs):
    master_out[...] = adam_tail(grad_own[...], w[...], 0.9 * m[...], 0.95 * v[...])[0]
    for s, grad in enumerate((grad_0, grad_1)):
        nw, nf, ns = adam_tail(grad[...], held[0, s], held[1, s], held[2, s])
        hw[s] = nw.astype(jnp.bfloat16)
        hf[s] = nf
        hs[s] = ns


def finish(grads, w, m, v, held):
    rows, cols = w.shape
    step = 112
    flat = pl.BlockSpec((step, cols), lambda i: (i, 0))
    pair = pl.BlockSpec((2, step, cols), lambda i: (0, i, 0))
    return pl.pallas_call(
        adam_kernel,
        grid=(rows // step,),
        in_specs=[flat] * 6
        + [pl.BlockSpec((3, 2, step, cols), lambda i: (0, 0, i, 0))],
        out_specs=[flat, pair, pair, pair],
        out_shape=[
            jax.ShapeDtypeStruct((rows, cols), F32),
            jax.ShapeDtypeStruct((2, rows, cols), jnp.bfloat16),
            jax.ShapeDtypeStruct((2, rows, cols), F32),
            jax.ShapeDtypeStruct((2, rows, cols), F32),
        ],
        compiler_params=pltpu.CompilerParams(vmem_limit_bytes=26 << 20),
    )(*grads, w, m, v, held)


def body(
    saved_inputs,
    saved_cotangents,
    row_counts,
    old_slots,
    new_slots,
    master,
    first_moment,
    second_moment,
):
    expert_index = lax.axis_index("expert")
    data_index = lax.axis_index("dp")
    y, z = data_index // NZ, data_index % NZ
    x, core = expert_index // 2, expert_index % 2
    inputs = saved_inputs[0]
    cot = saved_cotangents[0]
    rows = inputs.shape[0]
    shard = master.shape[1]
    offsets = jnp.array([0, 3, 1, 2], jnp.int32)
    ids = old_slots.reshape(NX, 2, 2)[(x + offsets) % NX]
    ids = jnp.where(core == 0, ids, ids[:, ::-1]).transpose(1, 0, 2).reshape(16)
    mine_new = lax.dynamic_index_in_dim(new_slots, expert_index, 0, keepdims=False)
    targets = jnp.concatenate([expert_index[None].astype(jnp.int32), mine_new])
    table = jnp.where(ids[:, None] == targets[None, :], 0.125, 0.0).astype(F32)
    table = jnp.broadcast_to(table[:, :, None, None], (16, 3, 1, master.shape[2]))
    table = lax.optimization_barrier(table)

    here = jnp.stack([core, y, z])
    *part0, state = partial(
        0, here, row_counts[0], inputs, cot, shard, (master[0], first_moment[0], second_moment[0])
    )
    other_state = lax.ppermute(state, "expert", core_swap())
    small = [part0[2].astype(F16), part0[3].astype(F16)]
    small, other_state = lax.optimization_barrier((small, other_state))
    far_up = send(small[0], 1, True)
    raw_down = send(small[1], -1, True)
    pair = jnp.stack([state, other_state])
    beside = send_x(pair)

    cot, part0, pair = lax.optimization_barrier((cot, part0, pair))
    part1 = partial(1, here, row_counts[0], inputs, cot, shard)
    part1, far_up, raw_down = lax.optimization_barrier((part1, far_up, raw_down))
    far_down = send(part1[2].astype(F16), -1, True)
    both_up = send((part0[1] + far_up.astype(F32)).astype(F16), 1, True)
    far_down, both_up, part1_near = lax.optimization_barrier((far_down, both_up, part1[1]))
    raw_up = send(part1_near.astype(F16), 1, True)
    both_down = send((part1[3] + far_down.astype(F32)).astype(F16), -1, True)
    back = 8.0 * 2.0 / SCALE

    def swap(value):
        return lax.ppermute(value, "expert", core_swap())

    def spread(got):
        own = (jnp.sum(got.astype(F32), 0) * back).astype(F16)
        return [own] + [lax.ppermute(own, "expert", x_shift(d)) for d in (1, -1, 2)]

    beside, both_up = lax.optimization_barrier((beside, both_up))
    far_state = send_x(beside[0])
    cross_state = swap(beside)
    sum_a = (part0[0] + both_up.astype(F32) + raw_down.astype(F32)) * 0.5
    got_a = exchange(sum_a.astype(F16))
    got_a, both_down, raw_up, far_state, cross_state = lax.optimization_barrier(
        (got_a, both_down, raw_up, far_state, cross_state)
    )
    sum_b = (part1[0] + raw_up.astype(F32) + both_down.astype(F32)) * 0.5
    got_b = exchange(sum_b.astype(F16))
    same_a = spread(got_a)

    at = (mine_new // 2 - x) % NX
    twist = (mine_new % 2 != core).astype(jnp.int32)
    near = jnp.where((at == 3) == (core == 0), 2 + twist, 5 - twist)
    pick = jnp.where(at == 0, twist, jnp.where(at == 2, 6 + twist, near))
    held = prepare(pick, [pair, beside, cross_state], [far_state, swap(far_state)])
    got_b, same_a, held = lax.optimization_barrier((got_b, same_a, held))
    same_b = spread(got_b)
    other_a = [swap(v) for v in same_a]
    other_a, same_b = lax.optimization_barrier((other_a, same_b))

    def weighted(same, other, s, t):
        total = 0.0
        for k, g in enumerate(same + other):
            total = total + table[2 * k + s, t] * g.astype(F32)
        return total

    grads_a = [weighted(same_a, other_a, 0, t) for t in range(3)]
    grads_a = lax.optimization_barrier(grads_a)
    other_b = [lax.ppermute(v, "expert", core_swap()) for v in same_b]
    grads = [grads_a[t] + weighted(same_b, other_b, 1, t) for t in range(3)]
    new_master, held_w, held_first, held_second = finish(
        grads, master[0], first_moment[0], second_moment[0], held
    )
    return new_master[None], held_w, held_first, held_second


def solution(mesh):
    return jax.shard_map(
        body,
        mesh=mesh,
        in_specs=(
            P("expert", "dp", None),
            P("expert", "dp", None),
            P("expert", None, None),
            P(),
            P(),
            P("expert", "dp", None),
            P("expert", "dp", None),
            P("expert", "dp", None),
        ),
        out_specs=(
            P("expert", "dp", None),
            P("expert", "dp", None),
            P("expert", "dp", None),
            P("expert", "dp", None),
        ),
        check_vma=False,
    )
```

```python
import functools

import jax
import jax.numpy as jnp
from jax import lax
from jax.experimental import pallas as pl
from jax.experimental.pallas import tpu as pltpu
from jax.sharding import PartitionSpec as P

F16 = jnp.float16
F32 = jnp.float32
NY, NZ, NX = 4, 4, 4
WINDOW = 656
CHUNKS = ((0, 176), (176, 160), (336, 160), (496, 160))
SCALE = 64.0


def plane_shift(d, first):
    pairs = []
    for e in range(2 * NX):
        along_y = (e % 2 == 0) == first
        for j in range(NY * NZ):
            y, z = j // NZ, j % NZ
            to = ((y + d) % NY) * NZ + z if along_y else y * NZ + (z + d) % NZ
            pairs.append((e * NY * NZ + j, e * NY * NZ + to))
    return pairs


def send(value, d, first):
    return lax.ppermute(value, ("expert", "dp"), plane_shift(d, first))


def x_shift(d):
    return [(e, ((e // 2 + d) % NX) * 2 + e % 2) for e in range(2 * NX)]


def send_x(value):
    pairs = [(e, ((e // 2 + (1 if e % 2 == 0 else -1)) % NX) * 2 + e % 2) for e in range(2 * NX)]
    return lax.ppermute(value, "expert", pairs)


def core_swap():
    return [(e, e ^ 1) for e in range(2 * NX)]


def encode_state(w, m, v):
    root = jnp.exp2(0.125 * jnp.log2(jnp.clip(jnp.abs(m) * (1.0 / 0.75), 1e-30, 1.0)))
    qm = jnp.round(jnp.where(m < 0, -root, root) * 32767.0).astype(jnp.int32)
    qv = jnp.round(jnp.sqrt(jnp.clip(v * 5.0, 0.0, 1.0)) * 65535.0).astype(jnp.int32)
    return (w * 2.0**32).astype(jnp.int32), qm * 65536 + qv


def decode_moments(code):
    qm = lax.shift_right_arithmetic(code, jnp.int32(16)).astype(F32) * (1.0 / 32767.0)
    qv = (code & jnp.int32(0xFFFF)).astype(F32) * (1.0 / 65535.0)
    m2 = qm * qm
    m4 = m2 * m2
    m8 = m4 * m4 * 0.75
    return jnp.where(qm < 0, -m8, m8), qv * qv * 0.2


def partial_kernel(which, here, counts, x, c, *refs):
    if which == 0:
        owned, outs, state_out, refs = refs[:3], refs[3:7], refs[7], refs[8:]
        held, state, held_sems, state_sem = refs[7:]
    else:
        outs, refs = refs[:4], refs[4:]
    rows, plain, masked, total, load_sems, cot_sem, sems = refs[:7]
    step = pl.program_id(0)
    core, y, z = here[0], here[1], here[2]
    first, second = counts[y * NZ + z, 0], counts[y * NZ + z, 1]
    if which == 0:
        start, low, high = 0, 0, first
    else:
        start = pl.multiple_of(jnp.minimum(first // 16 * 16, x.shape[0] - WINDOW), 16)
        low, high = first - start, first + second - start
    shard = total.shape[2]
    width = rows.shape[2]
    slot = lax.rem(step, 2)

    def loads(i):
        column = pl.multiple_of(lax.rem(y + 2 + i, NY) * width, width)
        for k, (at, size) in enumerate(CHUNKS):
            yield pltpu.make_async_copy(
                x.at[pl.ds(start + at, size), pl.ds(column, width)],
                rows.at[i, pl.ds(at, size)],
                load_sems.at[i, k],
            )

    @pl.when(step == 0)
    def _():
        cot_load = pltpu.make_async_copy(c.at[pl.ds(start, WINDOW)], plain, cot_sem)
        cot_load.start()
        for copy in loads(0):
            copy.start()
        cot_load.wait()
        index = lax.broadcasted_iota(jnp.int32, masked.shape, 0)
        value = plain[...].astype(F32) * SCALE
        masked[...] = jnp.where((index >= low) & (index < high), value, 0.0).astype(jnp.bfloat16)
        for i in range(1, NY):
            for copy in loads(i):
                copy.start()
        if which == 0:
            for k in range(3):
                pltpu.make_async_copy(owned[k], held.at[k], held_sems.at[k]).start()

    if which == 0:

        @pl.when(step == 2)
        def _():
            for k in range(3):
                pltpu.make_async_copy(owned[k], held.at[k], held_sems.at[k]).wait()

            @pl.loop(0, shard, step=32)
            def _(at):
                part = pl.ds(pl.multiple_of(at, 32), 32)
                state[0, part], state[1, part] = encode_state(
                    held[0, part], held[1, part], held[2, part]
                )

            pltpu.make_async_copy(state, state_out, state_sem).start()

        @pl.when(step == NY - 1)
        def _():
            pltpu.make_async_copy(state, state_out, state_sem).wait()

    for copy in loads(step):
        copy.wait()

    def wait(slot):
        pltpu.make_async_copy(total.at[slot], outs[0], sems.at[slot]).wait()

    @pl.when(step >= 2)
    def _():
        wait(slot)

    product = lax.dot_general(
        rows[step], masked[...], (((0,), (0,)), ((), ())), preferred_element_type=F32
    )
    for b in range(NZ):
        total[slot, b] = product[b * shard : (b + 1) * shard]

    for d in range(4):

        @pl.when((core == 0) & (lax.rem(2 + step, NY) == d))
        def _():
            pltpu.make_async_copy(total.at[slot], outs[d], sems.at[slot]).start()

        @pl.when((core == 1) & (z == d))
        def _():
            for b in range(NZ):
                pltpu.make_async_copy(
                    total.at[slot, b], outs[(b - d) % NZ].at[lax.rem(y + 2 + step, NY)], sems.at[slot]
                ).start()

    @pl.when(step == NY - 1)
    def _():
        wait(1 - slot)
        wait(slot)


def partial(which, here, counts, inputs, cot, shard, owned=()):
    rows, width_d = inputs.shape
    width_h = cot.shape[1]
    block = width_d // NY
    piece = pltpu.HBM((4, shard, width_h), F32)
    out_shape = [piece] * 4
    scratch = [
        pltpu.VMEM((NY, WINDOW, block), jnp.bfloat16),
        pltpu.VMEM((WINDOW, width_h), jnp.bfloat16),
        pltpu.VMEM((WINDOW, width_h), jnp.bfloat16),
        pltpu.VMEM((2, NZ, shard, width_h), F32),
        pltpu.SemaphoreType.DMA((NY, len(CHUNKS))),
        pltpu.SemaphoreType.DMA,
        pltpu.SemaphoreType.DMA((2,)),
    ]
    if which == 0:
        out_shape = out_shape + [pltpu.HBM((2, shard, width_h), jnp.int32)]
        scratch = scratch + [
            pltpu.VMEM((3, shard, width_h), F32),
            pltpu.VMEM((2, shard, width_h), jnp.int32),
            pltpu.SemaphoreType.DMA((3,)),
            pltpu.SemaphoreType.DMA,
        ]
    operands = [pltpu.with_memory_space_constraint(v, pltpu.HBM) for v in (inputs, cot, *owned)]
    return pl.pallas_call(
        functools.partial(partial_kernel, which),
        grid_spec=pltpu.PrefetchScalarGridSpec(
            num_scalar_prefetch=2,
            grid=(NY,),
            in_specs=[pl.BlockSpec(memory_space=pl.ANY)] * len(operands),
            out_specs=[pl.BlockSpec(memory_space=pltpu.HBM)] * len(out_shape),
            scratch_shapes=scratch,
        ),
        out_shape=out_shape,
        compiler_params=pltpu.CompilerParams(vmem_limit_bytes=28 << 20),
        cost_estimate=pl.CostEstimate(flops=1 << 33, bytes_accessed=1 << 24, transcendentals=0),
    )(here, counts, *operands)


def exchange(total):
    groups = []
    for e in range(2 * NX):
        for fixed in range(4):
            members = [fixed * NZ + q if e % 2 == 0 else q * NZ + fixed for q in range(4)]
            groups.append([e * NY * NZ + j for j in members])
    return lax.all_to_all(total, ("expert", "dp"), 0, 0, axis_index_groups=groups, tiled=True)


def add_up(parts):
    return sum(p.astype(F32) for p in parts)


def prepare_kernel(pick, *refs):
    sources = [ref.at[i] for ref in refs[:3] for i in range(2)] + list(refs[3:5])
    held, state, sems = refs[5:]
    for s in range(2):
        for k in range(8):

            @pl.when(pick[s] == k)
            def _():
                pltpu.make_async_copy(sources[k], state.at[s], sems.at[s]).start()

    for s in range(2):
        pltpu.make_async_copy(sources[0], state.at[s], sems.at[s]).wait()

        @pl.loop(0, state.shape[2], step=32)
        def _(at):
            part = pl.ds(pl.multiple_of(at, 32), 32)
            m, v = decode_moments(state[s, 1, part])
            held[0, s, part] = state[s, 0, part].astype(F32) * 2.0**-32
            held[1, s, part] = 0.9 * m
            held[2, s, part] = 0.95 * v


def prepare(pick, pairs, singles):
    _, rows, cols = singles[0].shape
    sources = pairs + singles
    sources = [pltpu.with_memory_space_constraint(v, pltpu.HBM) for v in sources]
    return pl.pallas_call(
        prepare_kernel,
        grid_spec=pltpu.PrefetchScalarGridSpec(
            num_scalar_prefetch=1,
            grid=(1,),
            in_specs=[pl.BlockSpec(memory_space=pl.ANY)] * 5,
            out_specs=pl.BlockSpec((3, 2, rows, cols), lambda i, pick: (0, 0, 0, 0)),
            scratch_shapes=[
                pltpu.VMEM((2, 2, rows, cols), jnp.int32),
                pltpu.SemaphoreType.DMA((2,)),
            ],
        ),
        out_shape=jax.ShapeDtypeStruct((3, 2, rows, cols), F32),
        compiler_params=pltpu.CompilerParams(vmem_limit_bytes=16 << 20),
    )(pick, *sources)


def adam_tail(gradient, w, m_decayed, v_decayed):
    first_new = m_decayed + 0.1 * gradient
    second_new = v_decayed + 0.05 * gradient * gradient
    root = jnp.sqrt(second_new * (1.0 / (1.0 - 0.95**20))) + 1e-08
    corrected = first_new * (1.0 / (1.0 - 0.9**20)) / root
    return w - 0.001 * (corrected + 0.1 * w), first_new, second_new


def adam_kernel(grad_own, grad_0, grad_1, w, m, v, held, master_out, hw, hf, hs):
    master_out[...] = adam_tail(grad_own[...], w[...], 0.9 * m[...], 0.95 * v[...])[0]
    for s, grad in enumerate((grad_0, grad_1)):
        nw, nf, ns = adam_tail(grad[...], held[0, s], held[1, s], held[2, s])
        hw[s] = nw.astype(jnp.bfloat16)
        hf[s] = nf
        hs[s] = ns


def finish(grads, w, m, v, held):
    rows, cols = w.shape
    step = 112
    flat = pl.BlockSpec((step, cols), lambda i: (i, 0))
    pair = pl.BlockSpec((2, step, cols), lambda i: (0, i, 0))
    return pl.pallas_call(
        adam_kernel,
        grid=(rows // step,),
        in_specs=[flat] * 6
        + [pl.BlockSpec((3, 2, step, cols), lambda i: (0, 0, i, 0))],
        out_specs=[flat, pair, pair, pair],
        out_shape=[
            jax.ShapeDtypeStruct((rows, cols), F32),
            jax.ShapeDtypeStruct((2, rows, cols), jnp.bfloat16),
            jax.ShapeDtypeStruct((2, rows, cols), F32),
            jax.ShapeDtypeStruct((2, rows, cols), F32),
        ],
        compiler_params=pltpu.CompilerParams(vmem_limit_bytes=26 << 20),
    )(*grads, w, m, v, held)


def body(
    saved_inputs,
    saved_cotangents,
    row_counts,
    old_slots,
    new_slots,
    master,
    first_moment,
    second_moment,
):
    expert_index = lax.axis_index("expert")
    data_index = lax.axis_index("dp")
    y, z = data_index // NZ, data_index % NZ
    x, core = expert_index // 2, expert_index % 2
    inputs = saved_inputs[0]
    cot = saved_cotangents[0]
    rows = inputs.shape[0]
    shard = master.shape[1]
    offsets = jnp.array([0, 3, 1, 2], jnp.int32)
    ids = old_slots.reshape(NX, 2, 2)[(x + offsets) % NX]
    ids = jnp.where(core == 0, ids, ids[:, ::-1]).transpose(1, 0, 2).reshape(16)
    mine_new = lax.dynamic_index_in_dim(new_slots, expert_index, 0, keepdims=False)
    targets = jnp.concatenate([expert_index[None].astype(jnp.int32), mine_new])
    table = jnp.where(ids[:, None] == targets[None, :], 0.125, 0.0).astype(F32)
    table = jnp.broadcast_to(table[:, :, None, None], (16, 3, 1, master.shape[2]))
    table = lax.optimization_barrier(table)

    here = jnp.stack([core, y, z])
    *part0, state = partial(
        0, here, row_counts[0], inputs, cot, shard, (master[0], first_moment[0], second_moment[0])
    )
    other_state = lax.ppermute(state, "expert", core_swap())
    small = [part0[2].astype(F16), part0[3].astype(F16)]
    small, other_state = lax.optimization_barrier((small, other_state))
    far_up = send(small[0], 1, True)
    raw_down = send(small[1], -1, True)
    pair = jnp.stack([state, other_state])
    beside = send_x(pair)

    cot, part0, pair = lax.optimization_barrier((cot, part0, pair))
    part1 = partial(1, here, row_counts[0], inputs, cot, shard)
    part1, far_up, raw_down = lax.optimization_barrier((part1, far_up, raw_down))
    far_down = send(part1[2].astype(F16), -1, True)
    both_up = send((part0[1] + far_up.astype(F32)).astype(F16), 1, True)
    far_down, both_up, part1_near = lax.optimization_barrier((far_down, both_up, part1[1]))
    raw_up = send(part1_near.astype(F16), 1, True)
    both_down = send((part1[3] + far_down.astype(F32)).astype(F16), -1, True)
    back = 8.0 * 2.0 / SCALE

    def swap(value):
        return lax.ppermute(value, "expert", core_swap())

    def spread(got):
        own = (jnp.sum(got.astype(F32), 0) * back).astype(F16)
        return [own] + [lax.ppermute(own, "expert", x_shift(d)) for d in (1, -1, 2)]

    beside, both_up = lax.optimization_barrier((beside, both_up))
    far_state = send_x(beside[0])
    cross_state = swap(beside)
    sum_a = (part0[0] + both_up.astype(F32) + raw_down.astype(F32)) * 0.5
    got_a = exchange(sum_a.astype(F16))
    got_a, both_down, raw_up, far_state = lax.optimization_barrier(
        (got_a, both_down, raw_up, far_state)
    )
    sum_b = (part1[0] + raw_up.astype(F32) + both_down.astype(F32)) * 0.5
    got_b = exchange(sum_b.astype(F16))
    got_a, cross_state = lax.optimization_barrier((got_a, cross_state))
    same_a = spread(got_a)

    at = (mine_new // 2 - x) % NX
    twist = (mine_new % 2 != core).astype(jnp.int32)
    near = jnp.where((at == 3) == (core == 0), 2 + twist, 5 - twist)
    pick = jnp.where(at == 0, twist, jnp.where(at == 2, 6 + twist, near))
    held = prepare(pick, [pair, beside, cross_state], [far_state, swap(far_state)])
    got_b, same_a, held = lax.optimization_barrier((got_b, same_a, held))
    same_b = spread(got_b)
    other_a = [swap(v) for v in same_a]
    other_a, same_b = lax.optimization_barrier((other_a, same_b))

    def weighted(same, other, s, t):
        total = 0.0
        for k, g in enumerate(same + other):
            total = total + table[2 * k + s, t] * g.astype(F32)
        return total

    grads_a = [weighted(same_a, other_a, 0, t) for t in range(3)]
    grads_a = lax.optimization_barrier(grads_a)
    other_b = [lax.ppermute(v, "expert", core_swap()) for v in same_b]
    grads = [grads_a[t] + weighted(same_b, other_b, 1, t) for t in range(3)]
    new_master, held_w, held_first, held_second = finish(
        grads, master[0], first_moment[0], second_moment[0], held
    )
    return new_master[None], held_w, held_first, held_second


def solution(mesh):
    return jax.shard_map(
        body,
        mesh=mesh,
        in_specs=(
            P("expert", "dp", None),
            P("expert", "dp", None),
            P("expert", None, None),
            P(),
            P(),
            P("expert", "dp", None),
            P("expert", "dp", None),
            P("expert", "dp", None),
        ),
        out_specs=(
            P("expert", "dp", None),
            P("expert", "dp", None),
            P("expert", "dp", None),
            P("expert", "dp", None),
        ),
        check_vma=False,
    )
```

```python
import functools

import jax
import jax.numpy as jnp
from jax import lax
from jax.experimental import pallas as pl
from jax.experimental.pallas import tpu as pltpu
from jax.sharding import PartitionSpec as P

F16 = jnp.float16
F32 = jnp.float32
NY, NZ, NX = 4, 4, 4
WINDOW = 656
CHUNKS = ((0, 176), (176, 160), (336, 160), (496, 160))
SCALE = 64.0


def plane_shift(d, first):
    pairs = []
    for e in range(2 * NX):
        along_y = (e % 2 == 0) == first
        for j in range(NY * NZ):
            y, z = j // NZ, j % NZ
            to = ((y + d) % NY) * NZ + z if along_y else y * NZ + (z + d) % NZ
            pairs.append((e * NY * NZ + j, e * NY * NZ + to))
    return pairs


def send(value, d, first):
    return lax.ppermute(value, ("expert", "dp"), plane_shift(d, first))


def x_shift(d):
    return [(e, ((e // 2 + d) % NX) * 2 + e % 2) for e in range(2 * NX)]


def send_x(value):
    pairs = [(e, ((e // 2 + (1 if e % 2 == 0 else -1)) % NX) * 2 + e % 2) for e in range(2 * NX)]
    return lax.ppermute(value, "expert", pairs)


def core_swap():
    return [(e, e ^ 1) for e in range(2 * NX)]


def encode_state(w, m, v):
    root = jnp.exp2(0.125 * jnp.log2(jnp.clip(jnp.abs(m) * (1.0 / 0.75), 1e-30, 1.0)))
    qm = jnp.round(jnp.where(m < 0, -root, root) * 32767.0).astype(jnp.int32)
    qv = jnp.round(jnp.sqrt(jnp.clip(v * 5.0, 0.0, 1.0)) * 65535.0).astype(jnp.int32)
    return (w * 2.0**32).astype(jnp.int32), qm * 65536 + qv


def decode_moments(code):
    qm = lax.shift_right_arithmetic(code, jnp.int32(16)).astype(F32) * (1.0 / 32767.0)
    qv = (code & jnp.int32(0xFFFF)).astype(F32) * (1.0 / 65535.0)
    m2 = qm * qm
    m4 = m2 * m2
    m8 = m4 * m4 * 0.75
    return jnp.where(qm < 0, -m8, m8), qv * qv * 0.2


def partial_kernel(which, here, counts, x, c, *refs):
    if which == 0:
        owned, outs, state_out, refs = refs[:3], refs[3:7], refs[7], refs[8:]
        held, state, held_sems, state_sem = refs[7:]
    else:
        outs, refs = refs[:4], refs[4:]
    rows, plain, masked, total, load_sems, cot_sem, sems = refs[:7]
    step = pl.program_id(0)
    core, y, z = here[0], here[1], here[2]
    first, second = counts[y * NZ + z, 0], counts[y * NZ + z, 1]
    if which == 0:
        start, low, high = 0, 0, first
    else:
        start = pl.multiple_of(jnp.minimum(first // 16 * 16, x.shape[0] - WINDOW), 16)
        low, high = first - start, first + second - start
    shard = total.shape[2]
    width = rows.shape[2]
    slot = lax.rem(step, 2)

    def loads(i):
        column = pl.multiple_of(lax.rem(y + 2 + i, NY) * width, width)
        for k, (at, size) in enumerate(CHUNKS):
            yield pltpu.make_async_copy(
                x.at[pl.ds(start + at, size), pl.ds(column, width)],
                rows.at[i, pl.ds(at, size)],
                load_sems.at[i, k],
            )

    @pl.when(step == 0)
    def _():
        cot_load = pltpu.make_async_copy(c.at[pl.ds(start, WINDOW)], plain, cot_sem)
        cot_load.start()
        for copy in loads(0):
            copy.start()
        cot_load.wait()
        index = lax.broadcasted_iota(jnp.int32, masked.shape, 0)
        value = plain[...].astype(F32) * SCALE
        masked[...] = jnp.where((index >= low) & (index < high), value, 0.0).astype(jnp.bfloat16)
        for i in range(1, NY):
            for copy in loads(i):
                copy.start()
        if which == 0:
            for k in range(3):
                pltpu.make_async_copy(owned[k], held.at[k], held_sems.at[k]).start()

    if which == 0:

        @pl.when(step == 2)
        def _():
            for k in range(3):
                pltpu.make_async_copy(owned[k], held.at[k], held_sems.at[k]).wait()

            @pl.loop(0, shard, step=32)
            def _(at):
                part = pl.ds(pl.multiple_of(at, 32), 32)
                state[0, part], state[1, part] = encode_state(
                    held[0, part], held[1, part], held[2, part]
                )

            pltpu.make_async_copy(state, state_out, state_sem).start()

        @pl.when(step == NY - 1)
        def _():
            pltpu.make_async_copy(state, state_out, state_sem).wait()

    for copy in loads(step):
        copy.wait()

    def wait(slot):
        pltpu.make_async_copy(total.at[slot], outs[0], sems.at[slot]).wait()

    @pl.when(step >= 2)
    def _():
        wait(slot)

    product = lax.dot_general(
        rows[step], masked[...], (((0,), (0,)), ((), ())), preferred_element_type=F32
    )
    for b in range(NZ):
        total[slot, b] = product[b * shard : (b + 1) * shard]

    for d in range(4):

        @pl.when((core == 0) & (lax.rem(2 + step, NY) == d))
        def _():
            pltpu.make_async_copy(total.at[slot], outs[d], sems.at[slot]).start()

        @pl.when((core == 1) & (z == d))
        def _():
            for b in range(NZ):
                pltpu.make_async_copy(
                    total.at[slot, b], outs[(b - d) % NZ].at[lax.rem(y + 2 + step, NY)], sems.at[slot]
                ).start()

    @pl.when(step == NY - 1)
    def _():
        wait(1 - slot)
        wait(slot)


def partial(which, here, counts, inputs, cot, shard, owned=()):
    rows, width_d = inputs.shape
    width_h = cot.shape[1]
    block = width_d // NY
    piece = pltpu.HBM((4, shard, width_h), F32)
    out_shape = [piece] * 4
    scratch = [
        pltpu.VMEM((NY, WINDOW, block), jnp.bfloat16),
        pltpu.VMEM((WINDOW, width_h), jnp.bfloat16),
        pltpu.VMEM((WINDOW, width_h), jnp.bfloat16),
        pltpu.VMEM((2, NZ, shard, width_h), F32),
        pltpu.SemaphoreType.DMA((NY, len(CHUNKS))),
        pltpu.SemaphoreType.DMA,
        pltpu.SemaphoreType.DMA((2,)),
    ]
    if which == 0:
        out_shape = out_shape + [pltpu.HBM((2, shard, width_h), jnp.int32)]
        scratch = scratch + [
            pltpu.VMEM((3, shard, width_h), F32),
            pltpu.VMEM((2, shard, width_h), jnp.int32),
            pltpu.SemaphoreType.DMA((3,)),
            pltpu.SemaphoreType.DMA,
        ]
    operands = [pltpu.with_memory_space_constraint(v, pltpu.HBM) for v in (inputs, cot, *owned)]
    return pl.pallas_call(
        functools.partial(partial_kernel, which),
        grid_spec=pltpu.PrefetchScalarGridSpec(
            num_scalar_prefetch=2,
            grid=(NY,),
            in_specs=[pl.BlockSpec(memory_space=pl.ANY)] * len(operands),
            out_specs=[pl.BlockSpec(memory_space=pltpu.HBM)] * len(out_shape),
            scratch_shapes=scratch,
        ),
        out_shape=out_shape,
        compiler_params=pltpu.CompilerParams(vmem_limit_bytes=28 << 20),
        cost_estimate=pl.CostEstimate(flops=1 << 33, bytes_accessed=1 << 24, transcendentals=0),
    )(here, counts, *operands)


def exchange(total):
    groups = []
    for e in range(2 * NX):
        for fixed in range(4):
            members = [fixed * NZ + q if e % 2 == 0 else q * NZ + fixed for q in range(4)]
            groups.append([e * NY * NZ + j for j in members])
    return lax.all_to_all(total, ("expert", "dp"), 0, 0, axis_index_groups=groups, tiled=True)


def add_up(parts):
    return sum(p.astype(F32) for p in parts)


def prepare_kernel(pick, *refs):
    sources = [ref.at[i] for ref in refs[:3] for i in range(2)] + list(refs[3:5])
    held, state, sems = refs[5:]
    for s in range(2):
        for k in range(8):

            @pl.when(pick[s] == k)
            def _():
                pltpu.make_async_copy(sources[k], state.at[s], sems.at[s]).start()

    for s in range(2):
        pltpu.make_async_copy(sources[0], state.at[s], sems.at[s]).wait()

        @pl.loop(0, state.shape[2], step=32)
        def _(at):
            part = pl.ds(pl.multiple_of(at, 32), 32)
            m, v = decode_moments(state[s, 1, part])
            held[0, s, part] = state[s, 0, part].astype(F32) * 2.0**-32
            held[1, s, part] = 0.9 * m
            held[2, s, part] = 0.95 * v


def prepare(pick, pairs, singles):
    _, rows, cols = singles[0].shape
    sources = pairs + singles
    sources = [pltpu.with_memory_space_constraint(v, pltpu.HBM) for v in sources]
    return pl.pallas_call(
        prepare_kernel,
        grid_spec=pltpu.PrefetchScalarGridSpec(
            num_scalar_prefetch=1,
            grid=(1,),
            in_specs=[pl.BlockSpec(memory_space=pl.ANY)] * 5,
            out_specs=pl.BlockSpec((3, 2, rows, cols), lambda i, pick: (0, 0, 0, 0)),
            scratch_shapes=[
                pltpu.VMEM((2, 2, rows, cols), jnp.int32),
                pltpu.SemaphoreType.DMA((2,)),
            ],
        ),
        out_shape=jax.ShapeDtypeStruct((3, 2, rows, cols), F32),
        compiler_params=pltpu.CompilerParams(vmem_limit_bytes=16 << 20),
    )(pick, *sources)


def adam_tail(gradient, w, m_decayed, v_decayed):
    first_new = m_decayed + 0.1 * gradient
    second_new = v_decayed + 0.05 * gradient * gradient
    root = jnp.sqrt(second_new * (1.0 / (1.0 - 0.95**20))) + 1e-08
    corrected = first_new * (1.0 / (1.0 - 0.9**20)) / root
    return w - 0.001 * (corrected + 0.1 * w), first_new, second_new


def adam_kernel(grad_own, grad_0, grad_1, w, m, v, held, master_out, hw, hf, hs):
    master_out[...] = adam_tail(grad_own[...], w[...], 0.9 * m[...], 0.95 * v[...])[0]
    for s, grad in enumerate((grad_0, grad_1)):
        nw, nf, ns = adam_tail(grad[...], held[0, s], held[1, s], held[2, s])
        hw[s] = nw.astype(jnp.bfloat16)
        hf[s] = nf
        hs[s] = ns


def finish(grads, w, m, v, held):
    rows, cols = w.shape
    step = 112
    flat = pl.BlockSpec((step, cols), lambda i: (i, 0))
    pair = pl.BlockSpec((2, step, cols), lambda i: (0, i, 0))
    return pl.pallas_call(
        adam_kernel,
        grid=(rows // step,),
        in_specs=[flat] * 6
        + [pl.BlockSpec((3, 2, step, cols), lambda i: (0, 0, i, 0))],
        out_specs=[flat, pair, pair, pair],
        out_shape=[
            jax.ShapeDtypeStruct((rows, cols), F32),
            jax.ShapeDtypeStruct((2, rows, cols), jnp.bfloat16),
            jax.ShapeDtypeStruct((2, rows, cols), F32),
            jax.ShapeDtypeStruct((2, rows, cols), F32),
        ],
        compiler_params=pltpu.CompilerParams(vmem_limit_bytes=26 << 20),
    )(*grads, w, m, v, held)


def body(
    saved_inputs,
    saved_cotangents,
    row_counts,
    old_slots,
    new_slots,
    master,
    first_moment,
    second_moment,
):
    expert_index = lax.axis_index("expert")
    data_index = lax.axis_index("dp")
    y, z = data_index // NZ, data_index % NZ
    x, core = expert_index // 2, expert_index % 2
    inputs = saved_inputs[0]
    cot = saved_cotangents[0]
    rows = inputs.shape[0]
    shard = master.shape[1]
    offsets = jnp.array([0, 3, 1, 2], jnp.int32)
    ids = old_slots.reshape(NX, 2, 2)[(x + offsets) % NX]
    ids = jnp.where(core == 0, ids, ids[:, ::-1]).transpose(1, 0, 2).reshape(16)
    mine_new = lax.dynamic_index_in_dim(new_slots, expert_index, 0, keepdims=False)
    targets = jnp.concatenate([expert_index[None].astype(jnp.int32), mine_new])
    table = jnp.where(ids[:, None] == targets[None, :], 0.125, 0.0).astype(F32)
    table = jnp.broadcast_to(table[:, :, None, None], (16, 3, 1, master.shape[2]))
    table = lax.optimization_barrier(table)

    here = jnp.stack([core, y, z])
    *part0, state = partial(
        0, here, row_counts[0], inputs, cot, shard, (master[0], first_moment[0], second_moment[0])
    )
    other_state = lax.ppermute(state, "expert", core_swap())
    small = [part0[2].astype(F16), part0[3].astype(F16)]
    small, other_state = lax.optimization_barrier((small, other_state))
    far_up = send(small[0], 1, True)
    raw_down = send(small[1], -1, True)
    pair = jnp.stack([state, other_state])
    beside = send_x(pair)

    cot, part0, pair = lax.optimization_barrier((cot, part0, pair))
    part1 = partial(1, here, row_counts[0], inputs, cot, shard)
    part1, far_up, raw_down = lax.optimization_barrier((part1, far_up, raw_down))
    far_down = send(part1[2].astype(F16), -1, True)
    both_up = send((part0[1] + far_up.astype(F32)).astype(F16), 1, True)
    far_down, both_up, part1_near = lax.optimization_barrier((far_down, both_up, part1[1]))
    raw_up = send(part1_near.astype(F16), 1, True)
    both_down = send((part1[3] + far_down.astype(F32)).astype(F16), -1, True)
    back = 8.0 * 2.0 / SCALE

    def swap(value):
        return lax.ppermute(value, "expert", core_swap())

    def spread(got):
        own = (jnp.sum(got.astype(F32), 0) * back).astype(F16)
        return [own] + [lax.ppermute(own, "expert", x_shift(d)) for d in (1, -1, 2)]

    beside, both_up = lax.optimization_barrier((beside, both_up))
    far_state = send_x(beside[0])
    cross_state = swap(beside)
    sum_a = (part0[0] + both_up.astype(F32) + raw_down.astype(F32)) * 0.5
    got_a = exchange(sum_a.astype(F16))
    got_a, both_down, raw_up, far_state = lax.optimization_barrier(
        (got_a, both_down, raw_up, far_state)
    )
    sum_b = (part1[0] + raw_up.astype(F32) + both_down.astype(F32)) * 0.5
    got_b = exchange(sum_b.astype(F16))
    got_a, cross_state = lax.optimization_barrier((got_a, cross_state))
    same_a = spread(got_a)

    at = (mine_new // 2 - x) % NX
    twist = (mine_new % 2 != core).astype(jnp.int32)
    near = jnp.where((at == 3) == (core == 0), 2 + twist, 5 - twist)
    pick = jnp.where(at == 0, twist, jnp.where(at == 2, 6 + twist, near))
    held = prepare(pick, [pair, beside, cross_state], [far_state, swap(far_state)])
    got_b, same_a, held = lax.optimization_barrier((got_b, same_a, held))
    same_b = spread(got_b)
    other_a = [swap(v) for v in same_a]
    swapped = swap(same_b[0])
    other_a, same_b, swapped = lax.optimization_barrier((other_a, same_b, swapped))

    def weighted(same, other, s, t):
        total = 0.0
        for k, g in enumerate(same + other):
            total = total + table[2 * k + s, t] * g.astype(F32)
        return total

    grads_a = [weighted(same_a, other_a, 0, t) for t in range(3)]
    grads_a = lax.optimization_barrier(grads_a)
    other_b = [swapped] + [swap(v) for v in same_b[1:]]
    grads = [grads_a[t] + weighted(same_b, other_b, 1, t) for t in range(3)]
    new_master, held_w, held_first, held_second = finish(
        grads, master[0], first_moment[0], second_moment[0], held
    )
    return new_master[None], held_w, held_first, held_second


def solution(mesh):
    return jax.shard_map(
        body,
        mesh=mesh,
        in_specs=(
            P("expert", "dp", None),
            P("expert", "dp", None),
            P("expert", None, None),
            P(),
            P(),
            P("expert", "dp", None),
            P("expert", "dp", None),
            P("expert", "dp", None),
        ),
        out_specs=(
            P("expert", "dp", None),
            P("expert", "dp", None),
            P("expert", "dp", None),
            P("expert", "dp", None),
        ),
        check_vma=False,
    )
```
